256 devices in a mesh: tm: 16 (over x, y), space: 16 (over z, core).
Axes of the slice: x: 4, y: 4, z: 8, core: 2. Of those that a mesh axis runs over, the one named last changes fastest.
Arguments:
- queries: bfloat16 [32, 32, 32, 2240], P('tm', 'space'), may hold values from -6 to 6
- keys: bfloat16 [32, 32, 32, 2240], P('tm', 'space'), may hold values from -6 to 6
- values: bfloat16 [32, 32, 32, 2240], P('tm', 'space'), may hold values from -6 to 6
- out_grad: bfloat16 [32, 32, 32, 2240], P('tm', 'space'), may hold values from -6 to 6
- block_start: int32 [32], P('tm'), may hold values 0 or 1
- conv_input: bfloat16 [32, 32, 32, 5632], P('tm', 'space'), may hold values from -6 to 6
- conv_grad: bfloat16 [32, 32, 32, 5632], P('tm', 'space'), may hold values from -6 to 6
- conv_weight: float32 [9, 5632], replicated, may hold values from -2 to 2
Outputs:
- query_grad: bfloat16 [32, 32, 32, 2240], P('tm', 'space')
- key_grad: bfloat16 [32, 32, 32, 2240], P('tm', 'space')
- value_grad: bfloat16 [32, 32, 32, 2240], P('tm', 'space')
- input_grad: bfloat16 [32, 32, 32, 5632], P('tm', 'space')
- kernel_grad: float32 [9, 5632], replicated
The draws below stay inside these ranges and needn't reach their ends.
All inputs are finite; a program needn't handle non-finite values. No bound on the sum of `block_start` on one device may be relied on, other than what follows from the above.
Results may differ from the reference program's by a relative error of at most 0.0088.
Values may be sent and summed in bfloat16 or wider, within the bound.
A program may use at most 128 MiB of HBM per device.

```python
import math
import jax
import jax.numpy as jnp
from jax import lax

HEADS = 20
HD = 112
CH = 5632
F_DEV = 2
W = 32
D = 2240
FRAMES = 32
H = 32
TOKENS = 32768


def touch_ends(drawn, key, smallest, largest):
    place = [jax.random.randint(jax.random.fold_in(key, axis), (), 0, length) for axis, length in enumerate(drawn.shape)]
    widest = drawn.shape.index(max(drawn.shape))
    beside = place[:widest] + [(place[widest] + 1) % drawn.shape[widest]] + place[widest + 1:]
    return drawn.at[tuple(place)].set(smallest).at[tuple(beside)].set(largest)


def block_levels(rng, extent, split, smallest, high):
    factor_of, own = 1.0, jax.random.fold_in(rng, 6)
    for dim, blocks in split:
        heights = jnp.exp(jax.random.uniform(jax.random.fold_in(own, dim), (blocks,), jnp.float32, smallest / len(split), high / len(split)))
        factor_of = factor_of * jnp.repeat(heights, extent[dim] // blocks).reshape([-1 if axis == dim else 1 for axis in range(len(extent))])
    return factor_of


def bell_draw(own_key, dims, width, most, pieces=(), kind=jnp.bfloat16):
    values = jax.random.normal(own_key, dims, jnp.float32) * width
    if len(pieces) > 0:
        values = block_levels(own_key, dims, pieces, -0.22, 0.18) * values
    return jnp.clip(values, min=-most, max=most).astype(kind)


def setup_inputs(seed: int = 0) -> dict:
    arg_keys = jax.random.split(jax.random.key(seed), 9)
    queries = bell_draw(arg_keys[0], (FRAMES, H, W, D), 1.0, 6.0, ((0, 16), (1, 16)))
    keys = bell_draw(arg_keys[1], (FRAMES, H, W, D), 1.0, 6.0, ((0, 16), (1, 16)))
    values = bell_draw(arg_keys[2], (FRAMES, H, W, D), 1.0, 6.0, ((0, 16), (1, 16)))
    out_grad = bell_draw(arg_keys[3], (FRAMES, H, W, D), 1.0, 6.0, ((0, 16), (1, 16)))
    block_start = touch_ends((jax.random.randint(arg_keys[4], (FRAMES,), 0, 2) < 1).astype(jnp.int32), jax.random.fold_in(arg_keys[4], 1), 0, 1)
    conv_input = bell_draw(arg_keys[5], (FRAMES, H, W, CH), 1.0, 6.0, ((0, 16), (1, 16)))
    conv_grad = bell_draw(arg_keys[6], (FRAMES, H, W, CH), 1.0, 6.0, ((0, 16), (1, 16)))
    conv_weight = bell_draw(arg_keys[7], (9, CH), 9 ** -0.5, 2.0, (), jnp.float32)
    return {"queries": queries, "keys": keys, "values": values, "out_grad": out_grad, "block_start": block_start, "conv_input": conv_input, "conv_grad": conv_grad, "conv_weight": conv_weight}


highest = lax.Precision.HIGHEST

def lifted(x):
    widened = x.astype(jnp.float32)
    return jnp.where(widened > 0, widened + 1.0, jnp.exp(jnp.minimum(widened, 0.0)))

def slopes(x):
    widened = x.astype(jnp.float32)
    return jnp.where(widened > 0, 1.0, jnp.exp(jnp.minimum(widened, 0.0)))

def visibility(block_start, count, span):
    position = jnp.arange(count, dtype=jnp.int32)
    starts = jnp.where(position % span == 0, 1, block_start).astype(jnp.int32)
    block_ids = jnp.cumsum(starts)
    return (block_ids[None, :] <= block_ids[:, None]).astype(jnp.float32)

def reference(queries, keys, values, out_grad, block_start, conv_input, conv_grad, conv_weight):
    head_shape = (FRAMES, H * W, HEADS, HD)
    q_feat = lifted(queries).astype(jnp.bfloat16).reshape(head_shape)
    k_feat = lifted(keys).astype(jnp.bfloat16).reshape(head_shape)
    v_heads = values.reshape(head_shape)

    def frame_state(items):
        kf, vf = items
        kf = kf.astype(jnp.float32)
        vf = vf.astype(jnp.float32)
        return (jnp.einsum('nhd,nhe->hde', kf, vf, precision=highest), lax.optimization_barrier(jnp.sum(kf, axis=0)))
    states, sums = lax.map(frame_state, (k_feat, v_heads))
    visible = visibility(block_start, FRAMES, F_DEV)
    seen_states = jnp.einsum('fg,ghde->fhde', visible, states, precision=highest)
    seen_sums = jnp.einsum('fg,ghd->fhd', visible, sums, precision=highest)

    def query_frame(items):
        qf, raw, dout, state, total = items
        q_wide = qf.astype(jnp.float32)
        grad_wide = dout.astype(jnp.float32)
        numer = jnp.einsum('nhd,hde->nhe', q_wide, state, precision=highest)
        denominator = jnp.einsum('nhd,hd->nh', q_wide, total, precision=highest)
        output = numer / denominator[..., None]
        numer_grad = (grad_wide / denominator[..., None]).astype(jnp.bfloat16)
        denom_grad = -lax.optimization_barrier(jnp.sum(grad_wide * output, axis=-1)) / denominator
        numer_wide = numer_grad.astype(jnp.float32)
        q_grad = jnp.einsum('nhe,hde->nhd', numer_wide, state, precision=highest) + denom_grad[..., None] * total[None]
        q_grad = (q_grad * slopes(raw)).astype(jnp.bfloat16)
        grad_state = jnp.einsum('nhd,nhe->hde', q_wide, numer_wide, precision=highest)
        grad_sum = jnp.einsum('nhd,nh->hd', q_wide, denom_grad, precision=highest)
        return (q_grad, grad_state, grad_sum)
    q_grads, grad_states, grad_sums = lax.map(query_frame, (q_feat, queries.reshape(head_shape), out_grad.reshape(head_shape), seen_states, seen_sums))
    seen_grads = jnp.einsum('fg,fhde->ghde', visible, grad_states, precision=highest)
    seen_gsums = jnp.einsum('fg,fhd->ghd', visible, grad_sums, precision=highest)

    def key_frame(items):
        kf, vf, raw, state, total = items
        k_wide = kf.astype(jnp.float32)
        v_wide = vf.astype(jnp.float32)
        k_grad = jnp.einsum('nhe,hde->nhd', v_wide, state, precision=highest) + total[None]
        v_grad = jnp.einsum('nhd,hde->nhe', k_wide, state, precision=highest)
        return ((k_grad * slopes(raw)).astype(jnp.bfloat16), v_grad.astype(jnp.bfloat16))
    k_grads, v_grads = lax.map(key_frame, (k_feat, v_heads, keys.reshape(head_shape), seen_grads, seen_gsums))
    out_shape = (FRAMES, H, W, HEADS * HD)

    def conv_frame(items):
        grad_frame, input_frame = items
        padded = jnp.pad(grad_frame.astype(jnp.float32), ((1, 1), (1, 1), (0, 0)))
        input_wide = input_frame.astype(jnp.float32)
        accum = jnp.zeros((H, W, CH), jnp.float32)
        kernel_rows = []
        for i in range(3):
            for j in range(3):
                window = padded[2 - i:2 - i + H, 2 - j:2 - j + W]
                accum = accum + conv_weight[3 * i + j] * window
                kernel_rows.append(lax.optimization_barrier(jnp.sum(window * input_wide, axis=(0, 1))))
        return (accum.astype(jnp.bfloat16), jnp.stack(kernel_rows))
    input_grad, kernel_parts = lax.map(conv_frame, (conv_grad, conv_input))
    kernel_grad = lax.optimization_barrier(jnp.sum(kernel_parts, axis=0)) * (1.0 / math.sqrt(TOKENS))
    return (q_grads.reshape(out_shape), k_grads.reshape(out_shape), v_grads.reshape(out_shape), input_grad, kernel_grad)
```

```python
import functools
import math

import jax
import jax.numpy as jnp
from jax import lax
from jax.experimental import pallas as pl
from jax.experimental.pallas import tpu as pltpu
from jax.sharding import PartitionSpec as P

HEADS = 20
HD = 112
LANES = 128
F32 = jnp.float32
BF16 = jnp.bfloat16
MESH = pl.DeviceIdType.MESH

CHUNK_HEADS = 10
NCH = 2
NZ = 8
NR = 4
ROWS = 144
HALF = 80
CROWS = NZ * ROWS
KROWS = 96
KTOT = NZ * KROWS
TOKENS = 128
HALFTOK = 64
GROUP = 5


def lifted(wide):
    return jnp.where(wide > 0, wide + 1.0, jnp.exp(jnp.minimum(wide, 0.0)))


def dot(a, b, ca, cb):
    return lax.dot_general(a, b, (((ca,), (cb,)), ((), ())), preferred_element_type=F32)


ORDER = (4, 3, 5, 2, 6, 1, 7)


class Place:
    def __init__(self):
        t = lax.axis_index("tm")
        s = lax.axis_index("space")
        self.t, self.s = t, s
        self.core = lax.rem(s, 2)
        self.z = lax.div(s, 2)
        self.x = lax.div(t, NR)
        self.y = lax.rem(t, NR)
        self.sibling = (t, s + 1 - 2 * self.core)
        self.up = (t, lax.rem(s + 2, 2 * NZ))
        self.down = (t, lax.rem(s + 2 * NZ - 2, 2 * NZ))
        self.ys = [(self.x * NR + lax.rem(self.y + k, NR), s) for k in (1, 2, 3)]
        self.xs = [(lax.rem(self.x + k, NR) * NR + self.y, s) for k in (1, 2, 3)]
        self.cross = (t, lax.rem(s + 2 * NZ - 1 + 2 * self.core, 2 * NZ))
        self.prev = (t, lax.rem(s + 2 * NZ - 1, 2 * NZ))
        self.next = (t, lax.rem(s + 1, 2 * NZ))


def low_lane(wide):
    return lax.broadcasted_iota(jnp.int32, wide.shape, 1) == HD + 1


def pack(wide):
    rounded = wide.astype(BF16).astype(F32)
    rest = pltpu.roll(wide - rounded, 1, 1)
    return jnp.where(low_lane(wide), wide + rest, rounded).astype(BF16)


def spread(wide):
    lane = lax.broadcasted_iota(jnp.int32, wide.shape, 1)
    return jnp.where((lane == HD + 1) | (lane == HD + 2), pltpu.roll(wide, 1, 1), wide)


class Sum:
    def __init__(self, at, core, bufs, rows):
        self.at, self.core, self.rows = at, core, rows
        self.pending = []
        for name, ref in bufs.items():
            setattr(self, name, ref)

    def sl(self, o, lo=0, n=None):
        n = self.rows if n is None else n
        return pl.ds(pl.multiple_of(o * self.rows + lo, 16), n)

    def remote(self, src, dst, ss, rr, dev):
        return pltpu.make_async_remote_copy(
            src_ref=src, dst_ref=dst, send_sem=ss, recv_sem=rr, device_id=dev, device_id_type=MESH
        )

    def exchange_copy(self):
        return self.remote(self.loc, self.xbuf, self.ex_s, self.ex_r, self.at.sibling)

    def go(self, make):
        make().start()
        self.pending.append(make)

    def drain(self):
        for make in self.pending:
            make().wait_send()

    def forward_copy(self, j):
        ref = self.forwarded(j)
        return self.remote(ref, ref, self.fw_s.at[j], self.fw_r.at[j], self.at.sibling)

    def finish(self):
        for j in range(self.forwards):
            self.forward_copy(j).wait_recv()


class Direct(Sum):
    forwards = NZ

    def __init__(self, at, core, bufs, rows, mode):
        super().__init__(at, core, bufs, rows)
        self.mode = mode

    def away(self, j):
        return lax.rem(self.at.z + j, NZ)

    def peer(self, j):
        return (self.at.t, lax.rem(self.at.s + 2 * j, 2 * NZ))

    def round(self, wide):
        return wide.astype(BF16) if self.mode == "sum" else pack(wide)

    def scatter_copy(self, j):
        return self.remote(
            self.send.at[self.sl(self.away(j))], self.recv.at[j - 1], self.rs_s.at[j - 1], self.rs_r.at[j - 1], self.peer(j)
        )

    def scatter(self):
        self.exchange_copy().wait_recv()
        self.send[...] = self.round(self.mine[...] + self.xbuf[...])
        for j in ORDER:
            self.go(functools.partial(self.scatter_copy, j))

    def tm_copy(self, axis, k):
        if axis == "y":
            return self.remote(self.ysend, self.yrecv.at[k], self.y_s.at[k], self.y_r.at[k], self.at.ys[k])
        return self.remote(self.xsend, self.xrecv.at[k], self.x_s.at[k], self.x_r.at[k], self.at.xs[k])

    def weight(self, place, k):
        if self.mode == "sum":
            return 1.0
        before = (place - (k + 1) >= 0).astype(F32)
        return before if self.mode == "prefix" else 1.0 - before

    def close(self):
        own = self.mine[self.sl(self.at.z)] + self.xbuf[self.sl(self.at.z)]
        for j in ORDER[::-1]:
            self.scatter_copy(j).wait_recv()
            own = own + self.recv[j - 1].astype(F32)
        self.own[...] = own
        self.ysend[...] = self.round(own)
        for k in (1, 0, 2):
            self.go(functools.partial(self.tm_copy, "y", k))

    def over_y(self):
        total = self.own[...]
        part = total
        for k in (0, 2, 1):
            self.tm_copy("y", k).wait_recv()
            got = self.yrecv[k].astype(F32)
            total = total + got
            part = part + self.weight(self.at.y, k) * got
        self.own[...] = part
        self.xsend[...] = self.round(total)
        for k in (1, 0, 2):
            self.go(functools.partial(self.tm_copy, "x", k))

    def over_x(self):
        part = self.own[...]
        for k in (0, 2, 1):
            self.tm_copy("x", k).wait_recv()
            part = part + self.weight(self.at.x, k) * self.xrecv[k].astype(F32)
        self.gbuf[self.sl(self.at.z)] = self.round(part)
        for j in ORDER:
            self.go(functools.partial(self.gather_copy, j))
        self.go(functools.partial(self.forward_copy, 0))

    def gather_copy(self, j):
        ref = self.gbuf.at[self.sl(self.at.z)]
        return self.remote(ref, ref, self.ag_s.at[j - 1], self.ag_r.at[j - 1], self.peer(j))

    def arrived_copy(self, j):
        ref = self.gbuf.at[self.sl(self.away(NZ - j))]
        return self.remote(ref, ref, self.ag_s.at[j - 1], self.ag_r.at[j - 1], self.peer(j))

    def forwarded(self, j):
        return self.gbuf.at[self.sl(self.away(NZ - j) if j else self.at.z)]

    def gather(self):
        for j in ORDER[::-1]:
            self.arrived_copy(j).wait_recv()
            self.go(functools.partial(self.forward_copy, j))


class Ring(Sum):
    forwards = 9

    def part(self, d, far):
        if not far:
            return 0, self.rows
        return (0, HALF) if d == 0 else (HALF, self.rows - HALF)

    def dev(self, d):
        return self.at.up if d == 0 else self.at.down

    def take(self):
        self.exchange_copy().wait_recv()
        self.acc[...] = self.mine[...] + self.xbuf[...]

    def scatter_copy(self, d, s):
        part = pl.ds(*self.part(d, s == 0))
        return self.remote(
            self.send.at[d, s, part], self.recv.at[d, s, part], self.rs_s.at[d, s], self.rs_r.at[d, s], self.dev(d)
        )

    def scatter(self, s):
        for d in (0, 1):
            o = lax.rem(self.at.z + (4 - s if d == 0 else 4 + s), NZ)
            lo, n = self.part(d, True)
            olo, on = self.part(1 - d, True)
            if s > 0:
                self.scatter_copy(d, s - 1).wait_recv()
            if s < 2:
                wide = self.acc[self.sl(o, lo, n)]
                if s == 1:
                    wide = wide + self.recv[d, 0, pl.ds(lo, n)].astype(F32)
                    self.send[d, 1, pl.ds(olo, on)] = pack(self.acc[self.sl(o, olo, on)])
                self.send[d, s, pl.ds(lo, n)] = pack(wide)
            else:
                self.send[d, s] = pack(self.acc[self.sl(o)] + self.recv[d, s - 1].astype(F32))
            self.go(functools.partial(self.scatter_copy, d, s))

    def close(self):
        self.scatter_copy(0, 3).wait_recv()
        self.scatter_copy(1, 3).wait_recv()
        own = self.acc[self.sl(self.at.z)] + self.recv[0, 3].astype(F32) + self.recv[1, 3].astype(F32)
        self.gbuf[self.sl(self.at.z)] = pack(own)

    def slice_from(self, d, s, far):
        o = lax.rem(self.at.z + (NZ - s if d == 0 else s), NZ)
        return self.gbuf.at[self.sl(o, *self.part(d, far))]

    def gather_copy(self, d, s):
        ref = self.slice_from(d, s, s == 3)
        return self.remote(ref, ref, self.ag_s.at[d, s], self.ag_r.at[d, s], self.dev(d))

    def arrived_copy(self, d, s):
        ref = self.slice_from(d, s + 1, s == 3)
        return self.remote(ref, ref, self.ag_s.at[d, s], self.ag_r.at[d, s], self.dev(d))

    def forwarded(self, j):
        s, d = (j + 1) // 2, (j + 1) % 2
        return self.slice_from(d, s, s == 4)

    def gather(self, s):
        if s > 0:
            for d in (0, 1):
                self.arrived_copy(d, s - 1).wait_recv()
        if s < 4:
            for d in (0, 1):
                self.go(functools.partial(self.gather_copy, d, s))
        for j in [0] if s == 0 else [2 * s - 1, 2 * s]:
            self.go(functools.partial(self.forward_copy, j))


def kernel(scale, *refs):
    (
        q_hbm, k_hbm, v_hbm, g_hbm, bs_ref, ci_hbm, cg_hbm, w_hbm,
        qo_hbm, ko_hbm, vo_hbm, io_hbm, wo_hbm,
        q_in, k_in, v_in, g_in, ci_in, cg_in, w_in,
        qo, ko, vo, io, wo,
        qp, kp, vp, gp, halo, ktaps,
        loc, xbuf, gbuf,
        dsend, drecv, down, dysend, dyrecv, dxsend, dxrecv,
        racc, rsend, rrecv,
        kloc, kxbuf, kgbuf, ksend, krecv, kown, kysend, kyrecv, kxsend, kxrecv,
        in_sem, out_sem, halo_s, halo_r,
        ex_s, ex_r, drs_s, drs_r, dag_s, dag_r, y_s, y_r, x_s, x_r,
        rrs_s, rrs_r, rag_s, rag_r, fw_s, fw_r,
    ) = refs
    at = Place()
    first_core, second_core = at.core == 0, at.core == 1
    channels = io.shape[-1]
    tiles = channels // LANES

    barrier = pltpu.get_barrier_semaphore()
    others = [at.sibling, at.cross, *at.ys, *at.xs]
    others += [(at.t, lax.rem(at.s + 2 * j, 2 * NZ)) for j in range(1, NZ)]
    for dev in others:
        pl.semaphore_signal(barrier, inc=1, device_id=dev, device_id_type=MESH)

    loads = [
        pltpu.make_async_copy(src, dst, in_sem.at[i])
        for i, (src, dst) in enumerate(
            [(k_hbm, k_in), (v_hbm, v_in), (q_hbm, q_in), (g_hbm, g_in), (cg_hbm, cg_in), (ci_hbm, ci_in), (w_hbm, w_in)]
        )
    ]
    for load in loads:
        load.start()

    def direct(i):
        return Direct(
            at, 0,
            dict(
                loc=loc.at[i, 1], mine=loc.at[i, 0], xbuf=xbuf.at[i], gbuf=gbuf.at[i, 0], send=dsend.at[i], recv=drecv.at[i],
                own=down.at[i], ysend=dysend.at[i], yrecv=dyrecv.at[i], xsend=dxsend.at[i], xrecv=dxrecv.at[i],
                ex_s=ex_s.at[i], ex_r=ex_r.at[i], rs_s=drs_s.at[i], rs_r=drs_r.at[i], ag_s=dag_s.at[i], ag_r=dag_r.at[i],
                y_s=y_s.at[i], y_r=y_r.at[i], x_s=x_s.at[i], x_r=x_r.at[i], fw_s=fw_s.at[i], fw_r=fw_r.at[i],
            ),
            ROWS, "prefix" if i < NCH else "suffix",
        )

    def ring(i):
        return Ring(
            at, 1,
            dict(
                loc=loc.at[i, 0], mine=loc.at[i, 1], xbuf=xbuf.at[i], gbuf=gbuf.at[i, 1], acc=racc.at[i],
                send=rsend.at[i], recv=rrecv.at[i],
                ex_s=ex_s.at[i], ex_r=ex_r.at[i], rs_s=rrs_s.at[i], rs_r=rrs_r.at[i], ag_s=rag_s.at[i], ag_r=rag_r.at[i],
                fw_s=fw_s.at[i], fw_r=fw_r.at[i],
            ),
            ROWS,
        )

    directs = [direct(i) for i in range(2 * NCH)]
    rings = [ring(i) for i in range(2 * NCH)]
    i = 2 * NCH
    ksum = Direct(
        at, 1,
        dict(
            loc=kloc, mine=kloc, xbuf=kxbuf, gbuf=kgbuf, send=ksend, recv=krecv,
            own=kown, ysend=kysend, yrecv=kyrecv, xsend=kxsend, xrecv=kxrecv,
            ex_s=ex_s.at[i], ex_r=ex_r.at[i], rs_s=drs_s.at[i], rs_r=drs_r.at[i], ag_s=dag_s.at[i], ag_r=dag_r.at[i],
            y_s=y_s.at[i], y_r=y_r.at[i], x_s=x_s.at[i], x_r=x_r.at[i], fw_s=fw_s.at[i], fw_r=fw_r.at[i],
        ),
        KROWS, "sum",
    )

    lane = lax.broadcasted_iota(jnp.int32, (TOKENS, LANES), 1)
    ones = ((lane == HD) | (lane == HD + 1)).astype(F32).astype(BF16)
    zero = jnp.zeros((TOKENS, LANES), BF16)

    def prepare(src, dst, heads, fill, lift):
        for h in heads:
            part = src[:, h * HD : (h + 1) * HD]
            if lift:
                part = lifted(part.astype(F32)).astype(BF16)
            dst[h] = fill
            dst[h, :, 0:HD] = part

    for i in range(2 * NCH):
        for j in range(2):
            loc[i, j, CHUNK_HEADS * HD :, :] = jnp.zeros((CROWS - CHUNK_HEADS * HD, LANES), F32)
    kloc[tiles * 16 :, :] = jnp.zeros((KTOT - tiles * 16, LANES), F32)

    @pl.when(at.s == 0)
    def _():
        halo[0] = jnp.zeros(halo.shape[1:], BF16)

    @pl.when(at.s == 2 * NZ - 1)
    def _():
        halo[1] = jnp.zeros(halo.shape[1:], BF16)

    pl.semaphore_wait(barrier, len(others))

    def halo_copy(d, f):
        return pltpu.make_async_remote_copy(
            src_ref=cg_hbm.at[f, 1 - d],
            dst_ref=halo.at[d, f],
            send_sem=halo_s.at[d, f],
            recv_sem=halo_r.at[d, f],
            device_id=at.next if d == 0 else at.prev,
            device_id_type=MESH,
        )

    has_next, has_prev = at.s < 2 * NZ - 1, at.s > 0

    def halo_start(f):
        @pl.when(has_next)
        def _():
            halo_copy(0, f).start()

        @pl.when(has_prev)
        def _():
            halo_copy(1, f).start()

    def halo_wait(f):
        @pl.when(has_prev)
        def _():
            halo_copy(0, f).wait_recv()

        @pl.when(has_next)
        def _():
            halo_copy(1, f).wait_recv()

    halo_start(0)
    loads[0].wait()
    loads[1].wait()

    def head_rows(h, n):
        return pl.ds(pl.multiple_of(h * HD, 16), n)

    def exchange(i):
        @pl.when(first_core)
        def _():
            directs[i].exchange_copy().start()

        @pl.when(second_core)
        def _():
            rings[i].exchange_copy().start()

    def states(c):
        no_low = lane[:HD] != HD + 1

        def some(n, _):
            heads = [n * GROUP + u for u in range(GROUP)]
            ks = [kp[c * CHUNK_HEADS + h] for h in heads]
            vs = [vp[c * CHUNK_HEADS + h] for h in heads]
            both = [dot(k, v, 0, 0)[:HD] for k, v in zip(ks, vs)]
            lone = [dot(k[HALFTOK:], v[HALFTOK:], 0, 0)[:HD] for k, v in zip(ks, vs)]
            for h, b, l in zip(heads, both, lone):
                loc[c, 0, head_rows(h, HD)] = jnp.where(no_low, b, 0.0)
                loc[c, 1, head_rows(h, HD)] = jnp.where(no_low, l, 0.0)
            return 0

        lax.fori_loop(0, CHUNK_HEADS // GROUP, some, 0)
        exchange(c)

    chunk = [range(c * CHUNK_HEADS, (c + 1) * CHUNK_HEADS) for c in range(NCH)]
    for c in range(NCH):
        prepare(k_in, kp, chunk[c], zero, True)
        prepare(v_in, vp, chunk[c], ones, False)
        states(c)

    col = lax.broadcasted_iota(jnp.int32, (32, LANES), 0)
    not_first, not_last = col > 0, col < 31

    def conv_tile(f, n, _):
        at_lane = pl.ds(pl.multiple_of(n * LANES, LANES), LANES)
        taps = [w_in[t : t + 1, at_lane] for t in range(9)]
        sums9 = [None] * 9
        rows = [halo[0, f, :, at_lane], cg_in[f, 0, :, at_lane], cg_in[f, 1, :, at_lane], halo[1, f, :, at_lane]]
        outs = [None, None]
        inner = [ci_in[f, r, :, at_lane].astype(F32) for r in range(2)]
        for m in range(4):
            wide = rows[m].astype(F32)
            later = jnp.where(not_last, pltpu.roll(wide, 31, 0), 0.0)
            earlier = jnp.where(not_first, pltpu.roll(wide, 1, 0), 0.0)
            for r in range(2):
                i = r + 2 - m
                if 0 <= i <= 2:
                    for j, window in enumerate((later, wide, earlier)):
                        t = 3 * i + j
                        add = taps[t] * window
                        outs[r] = add if outs[r] is None else outs[r] + add
                        prod = window * inner[r]
                        prod = prod[0:8] + prod[8:16] + (prod[16:24] + prod[24:32])
                        sums9[t] = prod if sums9[t] is None else sums9[t] + prod
        for r in range(2):
            io[f, r, :, at_lane] = outs[r].astype(BF16)
        total = jnp.concatenate(
            [jnp.sum(a, axis=0, keepdims=True) for a in sums9] + [jnp.zeros((7, LANES), F32)], axis=0
        )
        place = pl.ds(pl.multiple_of(n * 16, 16), 16)
        if f == 0:
            ktaps[place] = total
        else:
            kloc[place] = ktaps[place] + total
        return 0

    def conv(f, a, b):
        lax.fori_loop(a, b, functools.partial(conv_tile, f), 0)

    def conv_done():
        pltpu.make_async_copy(io, io_hbm, out_sem.at[3]).start()

        @pl.when(first_core)
        def _():
            ksum.exchange_copy().start()

    bs = bs_ref[1].astype(F32)

    def queries(c):
        lanes = lane[:HALFTOK]

        def some(n, _):
            heads = [n * GROUP + u for u in range(GROUP)]
            whole = [(qp[c * CHUNK_HEADS + h], gp[c * CHUNK_HEADS + h]) for h in heads]
            states = []
            for h in heads:
                last = gbuf[c, 0, head_rows(h, LANES)].astype(F32)
                lone = gbuf[c, 1, head_rows(h, LANES)].astype(F32)
                first = pack(last - bs * lone).astype(F32)
                states.append((spread(first).astype(BF16), spread(last).astype(BF16)))
            parts = [
                (q[f * HALFTOK : (f + 1) * HALFTOK], g[f * HALFTOK : (f + 1) * HALFTOK].astype(F32), s[f])
                for (q, g), s in zip(whole, states)
                for f in range(2)
            ]
            numers = [dot(q, s, 1, 0) for q, _, s in parts]
            dns = []
            for (_, g, _), numer in zip(parts, numers):
                inv = 1.0 / (numer[:, HD : HD + 1] + numer[:, HD + 2 : HD + 3])
                dd = -(jnp.sum(g * numer, axis=1, keepdims=True) * inv) * inv
                hi = dd.astype(BF16).astype(F32)
                wide = jnp.where((lanes == HD) | (lanes == HD + 2), hi, g * inv)
                dns.append(jnp.where(lanes == HD + 1, dd - hi, wide).astype(BF16))
            grads = [
                (dot(dn, s, 1, 1) * jnp.minimum(q.astype(F32), 1.0)).astype(BF16) for (q, _, s), dn in zip(parts, dns)
            ]
            both = [
                dot(q, jnp.concatenate(dns[2 * u : 2 * u + 2], axis=0), 0, 0)[:HD] for u, (q, _) in enumerate(whole)
            ]
            lone = [dot(parts[2 * u][0], dns[2 * u], 0, 0)[:HD] for u in range(GROUP)]
            for u, h in enumerate(heads):
                loc[NCH + c, 0, head_rows(h, HD)] = both[u]
                loc[NCH + c, 1, head_rows(h, HD)] = lone[u]
                gp[c * CHUNK_HEADS + h] = jnp.concatenate(grads[2 * u : 2 * u + 2], axis=0)
            return 0

        lax.fori_loop(0, CHUNK_HEADS // GROUP, some, 0)
        exchange(NCH + c)

    def keys(c):
        def some(n, _):
            heads = [n * GROUP + u for u in range(GROUP)]
            whole = [(kp[c * CHUNK_HEADS + h], vp[c * CHUNK_HEADS + h]) for h in heads]
            states = []
            for h in heads:
                first = gbuf[NCH + c, 0, head_rows(h, LANES)]
                lone = gbuf[NCH + c, 1, head_rows(h, LANES)]
                states.append((first, pack(first.astype(F32) - bs * lone.astype(F32))))
            outs = []
            for (k, v), s in zip(whole, states):
                kg = jnp.concatenate(
                    [dot(v[f * HALFTOK : (f + 1) * HALFTOK], s[f], 1, 1) for f in range(2)], axis=0
                )
                vg = jnp.concatenate(
                    [dot(k[f * HALFTOK : (f + 1) * HALFTOK], s[f], 1, 0) for f in range(2)], axis=0
                )
                outs.append(((kg * jnp.minimum(k.astype(F32), 1.0)).astype(BF16), vg.astype(BF16)))
            for h, (kg, vg) in zip(heads, outs):
                kp[c * CHUNK_HEADS + h] = kg
                vp[c * CHUNK_HEADS + h] = vg
            return 0

        lax.fori_loop(0, CHUNK_HEADS // GROUP, some, 0)

    def write(src, dst, heads):
        for h in heads:
            dst[:, h * HD : (h + 1) * HD] = src[h, :, 0:HD]

    def prepare_queries():
        loads[2].wait()
        loads[3].wait()
        for c in range(NCH):
            prepare(q_in, qp, chunk[c], zero, True)
            prepare(g_in, gp, chunk[c], zero, False)

    def conv_loads():
        for n in (4, 5, 6):
            loads[n].wait()

    half = tiles // 2

    @pl.when(first_core)
    def _():
        a, b = directs[0], directs[1]
        a.scatter()
        b.scatter()
        prepare_queries()
        a.close()
        b.close()
        halo_start(1)
        conv_loads()
        halo_wait(0)
        conv(0, 0, half)
        a.over_y()
        b.over_y()
        conv(0, half, tiles)
        a.over_x()
        b.over_x()
        halo_wait(1)
        conv(1, 0, half)
        a.gather()
        b.gather()

    @pl.when(second_core)
    def _():
        a, b = rings[0], rings[1]
        a.take()
        b.take()
        prepare_queries()
        for s in range(4):
            a.scatter(s)
            b.scatter(s)
        halo_start(1)
        a.close()
        b.close()
        for s in range(5):
            if s == 1:
                conv_loads()
                halo_wait(0)
            if s >= 1:
                conv(0, tiles * (s - 1) // 4, tiles * s // 4)
            a.gather(s)
            b.gather(s)
        halo_wait(1)
        conv(1, 0, half)

    def finish(i):
        @pl.when(first_core)
        def _():
            rings[i].finish()

        @pl.when(second_core)
        def _():
            directs[i].finish()

    for c in range(NCH):
        finish(c)
        queries(c)

    @pl.when(first_core)
    def _():
        a, b = directs[NCH], directs[NCH + 1]
        a.scatter()
        b.scatter()
        conv(1, half, tiles)
        conv_done()
        a.close()
        b.close()
        write(gp, qo, chunk[0])
        a.over_y()
        b.over_y()
        write(gp, qo, chunk[1])
        pltpu.make_async_copy(qo, qo_hbm, out_sem.at[0]).start()
        a.over_x()
        b.over_x()
        a.gather()
        b.gather()

    @pl.when(second_core)
    def _():
        a, b = rings[NCH], rings[NCH + 1]
        a.take()
        b.take()
        conv(1, half, tiles)
        conv_done()
        ksum.scatter()
        for s in range(4):
            a.scatter(s)
            b.scatter(s)
        ksum.close()
        a.close()
        b.close()
        for s in range(5):
            a.gather(s)
            b.gather(s)
            if s == 0:
                ksum.over_y()
                write(gp, qo, chunk[0])
            if s == 1:
                ksum.over_x()
                write(gp, qo, chunk[1])
                pltpu.make_async_copy(qo, qo_hbm, out_sem.at[0]).start()
        ksum.gather()

    for c in range(NCH):
        finish(NCH + c)
        keys(c)
        write(kp, ko, chunk[c])
        write(vp, vo, chunk[c])
    pltpu.make_async_copy(ko, ko_hbm, out_sem.at[1]).start()
    pltpu.make_async_copy(vo, vo_hbm, out_sem.at[2]).start()

    @pl.when(first_core)
    def _():
        ksum.finish()

    for n in range(tiles):
        wo[:, n * LANES : (n + 1) * LANES] = kgbuf[n * 16 : n * 16 + 16].astype(F32)[:9] * scale
    pltpu.make_async_copy(wo, wo_hbm, out_sem.at[4]).start()

    @pl.when(first_core)
    def _():
        for s in directs:
            s.exchange_copy().wait_send()
            s.drain()
        ksum.exchange_copy().wait_send()

    @pl.when(second_core)
    def _():
        for s in rings:
            s.exchange_copy().wait_send()
            s.drain()
        ksum.drain()

    for f in range(2):

        @pl.when(has_next)
        def _():
            halo_copy(0, f).wait_send()

        @pl.when(has_prev)
        def _():
            halo_copy(1, f).wait_send()

    for i, (src, dst) in enumerate([(qo, qo_hbm), (ko, ko_hbm), (vo, vo_hbm), (io, io_hbm), (wo, wo_hbm)]):
        pltpu.make_async_copy(src, dst, out_sem.at[i]).wait()


def move(*refs):
    srcs, dsts, bufs, in_sem, out_sem = refs[:5], refs[5:10], refs[10:15], refs[15], refs[16]
    loads = [pltpu.make_async_copy(s, b, in_sem.at[i]) for i, (s, b) in enumerate(zip(srcs, bufs))]
    stores = [pltpu.make_async_copy(b, d, out_sem.at[i]) for i, (b, d) in enumerate(zip(bufs, dsts))]
    for load in loads:
        load.start()
    for load, store in zip(loads, stores):
        load.wait()
        store.start()
    for store in stores:
        store.wait()


def body(queries, keys, values, out_grad, block_start, conv_input, conv_grad, conv_weight):
    frames, rows, cols, width = queries.shape
    channels = conv_grad.shape[-1]
    tokens = frames * rows * cols
    all_tokens = tokens * lax.axis_size("tm") * lax.axis_size("space")
    flat = (tokens, width)
    conv_shape = conv_grad.shape
    n = 2 * NCH
    vm, dma = pltpu.VMEM, pltpu.SemaphoreType.DMA

    def tm_bufs(lead, rows_):
        return [
            vm((*lead, rows_, LANES), F32),
            vm((*lead, rows_, LANES), BF16),
            vm((*lead, 3, rows_, LANES), BF16),
            vm((*lead, rows_, LANES), BF16),
            vm((*lead, 3, rows_, LANES), BF16),
        ]

    shapes = (
        jax.ShapeDtypeStruct(flat, BF16),
        jax.ShapeDtypeStruct(flat, BF16),
        jax.ShapeDtypeStruct(flat, BF16),
        jax.ShapeDtypeStruct(conv_shape, BF16),
        jax.ShapeDtypeStruct(conv_weight.shape, F32),
    )
    outs = pl.pallas_call(
        functools.partial(kernel, 1.0 / math.sqrt(all_tokens)),
        out_shape=shapes,
        in_specs=[pl.BlockSpec(memory_space=pl.ANY)] * 4
        + [pl.BlockSpec(memory_space=pltpu.SMEM)]
        + [pl.BlockSpec(memory_space=pl.ANY)] * 3,
        out_specs=[pl.BlockSpec(memory_space=pl.ANY)] * 5,
        scratch_shapes=[
            *[vm(flat, BF16)] * 4,
            vm(conv_shape, BF16),
            vm(conv_shape, BF16),
            vm(conv_weight.shape, F32),
            *[vm(flat, BF16)] * 3,
            vm(conv_shape, BF16),
            vm(conv_weight.shape, F32),
            *[vm((HEADS, tokens, LANES), BF16)] * 4,
            vm((2, frames, cols, channels), BF16),
            vm((KTOT, LANES), F32),
            vm((n, 2, CROWS, LANES), F32),
            vm((n, CROWS, LANES), F32),
            vm((n, 2, CROWS, LANES), BF16),
            vm((n, CROWS, LANES), BF16),
            vm((n, NZ - 1, ROWS, LANES), BF16),
            *tm_bufs((n,), ROWS),
            vm((n, CROWS, LANES), F32),
            vm((n, 2, 4, ROWS, LANES), BF16),
            vm((n, 2, 4, ROWS, LANES), BF16),
            vm((KTOT, LANES), F32),
            vm((KTOT, LANES), F32),
            vm((KTOT, LANES), BF16),
            vm((KTOT, LANES), BF16),
            vm((NZ - 1, KROWS, LANES), BF16),
            *tm_bufs((), KROWS),
            dma((7,)), dma((5,)), dma((2, 2)), dma((2, 2)),
            dma((n + 1,)), dma((n + 1,)),
            dma((n + 1, NZ - 1)), dma((n + 1, NZ - 1)),
            dma((n + 1, NZ - 1)), dma((n + 1, NZ - 1)),
            dma((n + 1, 3)), dma((n + 1, 3)),
            dma((n + 1, 3)), dma((n + 1, 3)),
            dma((n, 2, 4)), dma((n, 2, 4)),
            dma((n, 2, 4)), dma((n, 2, 4)),
            dma((n + 1, 9)), dma((n + 1, 9)),
        ],
        compiler_params=pltpu.CompilerParams(
            collective_id=0, has_side_effects=True, vmem_limit_bytes=56 << 20
        ),
        cost_estimate=pl.CostEstimate(flops=500_000_000, bytes_accessed=9_000_000, transcendentals=600_000),
        name="block_backward",
    )(
        queries.reshape(flat),
        keys.reshape(flat),
        values.reshape(flat),
        out_grad.reshape(flat),
        block_start,
        conv_input,
        conv_grad,
        conv_weight,
    )
    outs = pl.pallas_call(
        move,
        out_shape=shapes,
        in_specs=[pl.BlockSpec(memory_space=pl.ANY)] * 5,
        out_specs=[pl.BlockSpec(memory_space=pl.ANY)] * 5,
        scratch_shapes=[*[vm(o.shape, o.dtype) for o in shapes], dma((5,)), dma((5,))],
        name="results",
    )(*outs)
    shape = (frames, rows, cols, width)
    return (outs[0].reshape(shape), outs[1].reshape(shape), outs[2].reshape(shape), outs[3], outs[4])


def solution(mesh):
    split = P("tm", "space", None, None)
    return jax.shard_map(
        body,
        mesh=mesh,
        in_specs=(split, split, split, split, P("tm"), split, split, P()),
        out_specs=(split, split, split, split, P()),
        check_vma=False,
    )
```

```python
import functools
import math

import jax
import jax.numpy as jnp
from jax import lax
from jax.experimental import pallas as pl
from jax.experimental.pallas import tpu as pltpu
from jax.sharding import PartitionSpec as P

HEADS = 20
HD = 112
LANES = 128
F32 = jnp.float32
BF16 = jnp.bfloat16
MESH = pl.DeviceIdType.MESH

CHUNK_HEADS = 10
NCH = 2
NZ = 8
NR = 4
ROWS = 144
HALF = 80
CROWS = NZ * ROWS
KROWS = 96
KTOT = NZ * KROWS
KHALF = 48
TOKENS = 128
HALFTOK = 64
GROUP = 5


def lifted(wide):
    return jnp.where(wide > 0, wide + 1.0, jnp.exp(jnp.minimum(wide, 0.0)))


def dot(a, b, ca, cb):
    return lax.dot_general(a, b, (((ca,), (cb,)), ((), ())), preferred_element_type=F32)


class Place:
    def __init__(self):
        t = lax.axis_index("tm")
        s = lax.axis_index("space")
        self.t, self.s = t, s
        self.core = lax.rem(s, 2)
        self.z = lax.div(s, 2)
        self.x = lax.div(t, NR)
        self.y = lax.rem(t, NR)
        self.sibling = (t, s + 1 - 2 * self.core)
        self.up = (t, lax.rem(s + 2, 2 * NZ))
        self.down = (t, lax.rem(s + 2 * NZ - 2, 2 * NZ))
        self.ys = [(self.x * NR + lax.rem(self.y + k, NR), s) for k in (1, 2, 3)]
        self.xs = [(lax.rem(self.x + k, NR) * NR + self.y, s) for k in (1, 2, 3)]
        self.cross = (t, lax.rem(s + 2 * NZ - 1 + 2 * self.core, 2 * NZ))
        self.prev = (t, lax.rem(s + 2 * NZ - 1, 2 * NZ))
        self.next = (t, lax.rem(s + 1, 2 * NZ))


def pack(wide, step):
    lane = lax.broadcasted_iota(jnp.int32, wide.shape, 1)
    rounded = wide.astype(BF16).astype(F32)
    rest = pltpu.roll(wide - rounded, step, 1)
    return jnp.where(lane == HD + step, wide + rest, rounded).astype(BF16)


class Sum:
    forwards = 9

    def slice_from(self, d, s, far):
        o = lax.rem(self.at.z + (NZ - s if d == 0 else s), NZ)
        return self.gbuf.at[self.sl(o, *self.part(d, far))]

    def part(self, d, far):
        if not far:
            return 0, self.rows
        return (0, self.half) if d == 0 else (self.half, self.rows - self.half)

    def peer(self, d, n):
        return (self.at.t, lax.rem(self.at.s + (2 * n if d == 0 else 2 * (NZ - n)), 2 * NZ))

    def away(self, d, n):
        return lax.rem(self.at.z + (n if d == 0 else NZ - n), NZ)

    def forwarded(self, j):
        s, d = (j + 1) // 2, (j + 1) % 2
        return self.slice_from(d, s, s == 4)

    def round(self, wide):
        return wide.astype(BF16) if self.step is None else pack(wide, self.step)

    def __init__(self, at, bufs, rows, half, step):
        self.at, self.rows, self.half, self.step = at, rows, half, step
        self.pending = []
        for name, ref in bufs.items():
            setattr(self, name, ref)

    def sl(self, o, lo=0, n=None):
        n = self.rows if n is None else n
        return pl.ds(pl.multiple_of(o * self.rows + lo, 16), n)

    def remote(self, src, dst, ss, rr, dev):
        return pltpu.make_async_remote_copy(
            src_ref=src, dst_ref=dst, send_sem=ss, recv_sem=rr, device_id=dev, device_id_type=MESH
        )

    def exchange_copy(self):
        return self.remote(self.loc, self.xbuf, self.ex_s, self.ex_r, self.at.sibling)

    def go(self, make):
        make().start()
        self.pending.append(make)

    def drain(self):
        for make in self.pending:
            make().wait_send()

    def forward_copy(self, j):
        ref = self.forwarded(j)
        return self.remote(ref, ref, self.fw_s.at[j], self.fw_r.at[j], self.at.sibling)

    def finish(self):
        for j in range(self.forwards):
            self.forward_copy(j).wait_recv()


class Tree(Sum):
    def __init__(self, at, bufs, rows, half, step, mode):
        super().__init__(at, bufs, rows, half, step)
        self.mode = mode

    def far_copy(self, d, n):
        lo, count = self.part(d, n == 4)
        return self.remote(
            self.send.at[self.sl(self.away(d, n), lo, count)],
            self.recv.at[d, n - 3, pl.ds(lo, count)],
            self.rs_s.at[d, n - 3],
            self.rs_r.at[d, n - 3],
            self.peer(d, n - 2),
        )

    def near_copy(self, d):
        return self.remote(
            self.send.at[self.sl(self.away(d, 1))], self.recv.at[d, 2], self.rs_s.at[d, 2], self.rs_r.at[d, 2], self.peer(d, 1)
        )

    def middle_copy(self, d):
        return self.remote(self.middle.at[d], self.recv.at[d, 3], self.rs_s.at[d, 3], self.rs_r.at[d, 3], self.peer(d, 2))

    def scatter(self):
        self.exchange_copy().wait_recv()
        self.send[...] = self.round(self.mine[...] + self.xbuf[...])
        for n in (4, 3):
            for d in (0, 1):
                self.go(functools.partial(self.far_copy, d, n))
        for d in (0, 1):
            self.go(functools.partial(self.near_copy, d))

    def own_part(self, o, lo=0, n=None):
        at = self.sl(o, lo, n)
        return self.mine[at] + self.xbuf[at]

    def relay(self):
        for d in (0, 1):
            self.far_copy(d, 3).wait_recv()
            self.far_copy(d, 4).wait_recv()
            o = self.away(d, 2)
            lo, n = self.part(d, True)
            at = pl.ds(lo, n)
            both = self.recv[d, 0, at].astype(F32) + self.recv[d, 1, at].astype(F32)
            self.middle[d, at] = self.round(self.own_part(o, lo, n) + both)
            lo, n = self.part(1 - d, True)
            at = pl.ds(lo, n)
            self.middle[d, at] = self.round(self.own_part(o, lo, n) + self.recv[d, 0, at].astype(F32))
            self.go(functools.partial(self.middle_copy, d))

    def tm_copy(self, axis, k):
        if axis == "y":
            return self.remote(self.ysend, self.yrecv.at[k], self.y_s.at[k], self.y_r.at[k], self.at.ys[k])
        return self.remote(self.xsend, self.xrecv.at[k], self.x_s.at[k], self.x_r.at[k], self.at.xs[k])

    def weight(self, place, k):
        if self.mode == "sum":
            return 1.0
        before = (place - (k + 1) >= 0).astype(F32)
        return before if self.mode == "prefix" else 1.0 - before

    def close(self):
        own = self.own_part(self.at.z)
        for d in (0, 1):
            self.near_copy(d).wait_recv()
            own = own + self.recv[d, 2].astype(F32)
        for d in (0, 1):
            self.middle_copy(d).wait_recv()
            own = own + self.recv[d, 3].astype(F32)
        if self.mode == "lone":
            self.publish(own)
            return
        self.own[...] = own
        self.ysend[...] = self.round(own)
        for k in (1, 0, 2):
            self.go(functools.partial(self.tm_copy, "y", k))

    def over_y(self):
        total = self.own[...]
        part = total
        for k in (0, 2, 1):
            self.tm_copy("y", k).wait_recv()
            got = self.yrecv[k].astype(F32)
            total = total + got
            part = part + self.weight(self.at.y, k) * got
        self.own[...] = part
        self.xsend[...] = self.round(total)
        for k in (1, 0, 2):
            self.go(functools.partial(self.tm_copy, "x", k))

    def over_x(self):
        part = self.own[...]
        for k in (0, 2, 1):
            self.tm_copy("x", k).wait_recv()
            part = part + self.weight(self.at.x, k) * self.xrecv[k].astype(F32)
        self.publish(part)

    def publish(self, own):
        self.gbuf[self.sl(self.at.z)] = self.round(own)
        for s in (2, 1):
            for d in (0, 1):
                self.go(functools.partial(self.gather_copy, d, s))
        self.go(functools.partial(self.forward_copy, 0))

    def gather_copy(self, d, s):
        ref = self.slice_from(d, 0 if s < 3 else 2, s == 4)
        return self.remote(ref, ref, self.ag_s.at[d, s - 1], self.ag_r.at[d, s - 1], self.peer(d, s if s < 3 else s - 2))

    def arrived_copy(self, d, s):
        ref = self.slice_from(d, s, s == 4)
        return self.remote(ref, ref, self.ag_s.at[d, s - 1], self.ag_r.at[d, s - 1], self.peer(d, 1))

    def pass_on(self):
        for d in (0, 1):
            self.arrived_copy(d, 2).wait_recv()
            for s in (4, 3):
                self.go(functools.partial(self.gather_copy, d, s))
        for s in (2, 1):
            for d in (0, 1):
                if s == 1:
                    self.arrived_copy(d, 1).wait_recv()
                self.go(functools.partial(self.forward_copy, 2 * s - 1 + d))

    def gather(self):
        for s in (3, 4):
            for d in (0, 1):
                self.arrived_copy(d, s).wait_recv()
                self.go(functools.partial(self.forward_copy, 2 * s - 1 + d))


def kernel(scale, *refs):
    (
        q_hbm, k_hbm, v_hbm, g_hbm, bs_ref, ci_hbm, cg_hbm, w_hbm,
        qo, ko, vo, io, wo,
        q_in, k_in, v_in, g_in, ci_in, cg_in, w_in,
        qp, kp, vp, gp, halo, ktaps,
        loc, xbuf, gbuf,
        dsend, drecv, dmid, down, dysend, dyrecv, dxsend, dxrecv,
        kloc, kxbuf, kgbuf, ksend, krecv, kmid, kown, kysend, kyrecv, kxsend, kxrecv,
        in_sem, halo_s, halo_r,
        ex_s, ex_r, drs_s, drs_r, dag_s, dag_r, y_s, y_r, x_s, x_r,
        fw_s, fw_r,
    ) = refs
    at = Place()
    first_core, second_core = at.core == 0, at.core == 1
    channels = io.shape[-1]
    tiles = channels // LANES

    barrier = pltpu.get_barrier_semaphore()
    others = [at.sibling, at.cross, *at.ys, *at.xs]
    others += [(at.t, lax.rem(at.s + 2 * j, 2 * NZ)) for j in (1, 2, NZ - 2, NZ - 1)]
    for dev in others:
        pl.semaphore_signal(barrier, inc=1, device_id=dev, device_id_type=MESH)

    loads = [
        pltpu.make_async_copy(src, dst, in_sem.at[i])
        for i, (src, dst) in enumerate(
            [(k_hbm, k_in), (v_hbm, v_in), (q_hbm, q_in), (g_hbm, g_in), (cg_hbm, cg_in), (ci_hbm, ci_in), (w_hbm, w_in)]
        )
    ]
    for load in loads[:2]:
        load.start()

    def tree(i, which, mode):
        return Tree(
            at,
            dict(
                loc=loc.at[i, 1 - which], mine=loc.at[i, which], xbuf=xbuf.at[i], gbuf=gbuf.at[i, which],
                send=dsend.at[i], recv=drecv.at[i], middle=dmid.at[i],
                own=down.at[i], ysend=dysend.at[i], yrecv=dyrecv.at[i], xsend=dxsend.at[i], xrecv=dxrecv.at[i],
                ex_s=ex_s.at[i], ex_r=ex_r.at[i], rs_s=drs_s.at[i], rs_r=drs_r.at[i], ag_s=dag_s.at[i], ag_r=dag_r.at[i],
                y_s=y_s.at[i], y_r=y_r.at[i], x_s=x_s.at[i], x_r=x_r.at[i], fw_s=fw_s.at[i], fw_r=fw_r.at[i],
            ),
            ROWS, HALF, 2 if i < NCH else 1, mode,
        )

    pairs = [tree(i, 0, "prefix" if i < NCH else "suffix") for i in range(2 * NCH)]
    lones = [tree(i, 1, "lone") for i in range(2 * NCH)]
    i = 2 * NCH
    ksum = Tree(
        at,
        dict(
            loc=kloc, mine=kloc, xbuf=kxbuf, gbuf=kgbuf, send=ksend, recv=krecv, middle=kmid,
            own=kown, ysend=kysend, yrecv=kyrecv, xsend=kxsend, xrecv=kxrecv,
            ex_s=ex_s.at[i], ex_r=ex_r.at[i], rs_s=drs_s.at[i], rs_r=drs_r.at[i], ag_s=dag_s.at[i], ag_r=dag_r.at[i],
            y_s=y_s.at[i], y_r=y_r.at[i], x_s=x_s.at[i], x_r=x_r.at[i], fw_s=fw_s.at[i], fw_r=fw_r.at[i],
        ),
        KROWS, KHALF, None, "sum",
    )

    lane = lax.broadcasted_iota(jnp.int32, (TOKENS, LANES), 1)
    ones = ((lane == HD) | (lane == HD + 1)).astype(F32).astype(BF16)
    zero = jnp.zeros((TOKENS, LANES), BF16)

    def prepare(src, dst, heads, fill, lift):
        for h in heads:
            part = src[:, h * HD : (h + 1) * HD]
            if lift:
                part = lifted(part.astype(F32)).astype(BF16)
            dst[h] = fill
            dst[h, :, 0:HD] = part

    for i in range(2 * NCH):
        for j in range(2):
            loc[i, j, CHUNK_HEADS * HD :, :] = jnp.zeros((CROWS - CHUNK_HEADS * HD, LANES), F32)
    kloc[tiles * 16 :, :] = jnp.zeros((KTOT - tiles * 16, LANES), F32)

    @pl.when(at.s == 0)
    def _():
        halo[0] = jnp.zeros(halo.shape[1:], BF16)

    @pl.when(at.s == 2 * NZ - 1)
    def _():
        halo[1] = jnp.zeros(halo.shape[1:], BF16)

    pl.semaphore_wait(barrier, len(others))

    def halo_copy(d, f):
        return pltpu.make_async_remote_copy(
            src_ref=cg_hbm.at[f, 1 - d],
            dst_ref=halo.at[d, f],
            send_sem=halo_s.at[d, f],
            recv_sem=halo_r.at[d, f],
            device_id=at.next if d == 0 else at.prev,
            device_id_type=MESH,
        )

    has_next, has_prev = at.s < 2 * NZ - 1, at.s > 0

    def halo_start(f):
        @pl.when(has_next)
        def _():
            halo_copy(0, f).start()

        @pl.when(has_prev)
        def _():
            halo_copy(1, f).start()

    def halo_wait(f):
        @pl.when(has_prev)
        def _():
            halo_copy(0, f).wait_recv()

        @pl.when(has_next)
        def _():
            halo_copy(1, f).wait_recv()

    halo_start(0)
    loads[0].wait()
    loads[1].wait()
    for load in loads[2:]:
        load.start()

    def head_rows(h, n):
        return pl.ds(pl.multiple_of(h * HD, 16), n)

    def exchange(i):
        @pl.when(first_core)
        def _():
            pairs[i].exchange_copy().start()

        @pl.when(second_core)
        def _():
            lones[i].exchange_copy().start()

    def states(c):
        def some(n, _):
            heads = [n * GROUP + u for u in range(GROUP)]
            ks = [kp[c * CHUNK_HEADS + h] for h in heads]
            vs = [vp[c * CHUNK_HEADS + h] for h in heads]
            both = [dot(k, v, 0, 0)[:HD] for k, v in zip(ks, vs)]
            lone = [dot(k[HALFTOK:], v[HALFTOK:], 0, 0)[:HD] for k, v in zip(ks, vs)]
            for h, b, l in zip(heads, both, lone):
                loc[c, 0, head_rows(h, HD)] = b
                loc[c, 1, head_rows(h, HD)] = l
            return 0

        lax.fori_loop(0, CHUNK_HEADS // GROUP, some, 0)
        exchange(c)

    chunk = [range(c * CHUNK_HEADS, (c + 1) * CHUNK_HEADS) for c in range(NCH)]
    for c in range(NCH):
        prepare(k_in, kp, chunk[c], zero, True)
        prepare(v_in, vp, chunk[c], ones, False)
        states(c)

    col = lax.broadcasted_iota(jnp.int32, (32, LANES), 0)
    not_first, not_last = col > 0, col < 31

    def conv_tile(f, n, _):
        at_lane = pl.ds(pl.multiple_of(n * LANES, LANES), LANES)
        taps = [w_in[t : t + 1, at_lane] for t in range(9)]
        sums9 = [None] * 9
        rows = [halo[0, f, :, at_lane], cg_in[f, 0, :, at_lane], cg_in[f, 1, :, at_lane], halo[1, f, :, at_lane]]
        outs = [None, None]
        inner = [ci_in[f, r, :, at_lane].astype(F32) for r in range(2)]
        for m in range(4):
            wide = rows[m].astype(F32)
            later = jnp.where(not_last, pltpu.roll(wide, 31, 0), 0.0)
            earlier = jnp.where(not_first, pltpu.roll(wide, 1, 0), 0.0)
            for r in range(2):
                i = r + 2 - m
                if 0 <= i <= 2:
                    for j, window in enumerate((later, wide, earlier)):
                        t = 3 * i + j
                        add = taps[t] * window
                        outs[r] = add if outs[r] is None else outs[r] + add
                        prod = window * inner[r]
                        prod = prod[0:8] + prod[8:16] + (prod[16:24] + prod[24:32])
                        sums9[t] = prod if sums9[t] is None else sums9[t] + prod
        for r in range(2):
            io[f, r, :, at_lane] = outs[r].astype(BF16)
        total = jnp.concatenate(
            [jnp.sum(a, axis=0, keepdims=True) for a in sums9] + [jnp.zeros((7, LANES), F32)], axis=0
        )
        place = pl.ds(pl.multiple_of(n * 16, 16), 16)
        if f == 0:
            ktaps[place] = total
        else:
            kloc[place] = ktaps[place] + total
        return 0

    def conv(f, a, b):
        lax.fori_loop(a, b, functools.partial(conv_tile, f), 0)

    bs = bs_ref[1].astype(F32)

    def queries(c, n):
        lanes = lane[:HALFTOK]

        def some(n, _):
            heads = [n * GROUP + u for u in range(GROUP)]
            whole = [(qp[c * CHUNK_HEADS + h], gp[c * CHUNK_HEADS + h]) for h in heads]
            states = []
            for h in heads:
                last = gbuf[c, 0, head_rows(h, LANES)]
                lone = gbuf[c, 1, head_rows(h, LANES)]
                states.append((pack(last.astype(F32) - bs * lone.astype(F32), 2), last))
            parts = [
                (q[f * HALFTOK : (f + 1) * HALFTOK], g[f * HALFTOK : (f + 1) * HALFTOK].astype(F32), s[f])
                for (q, g), s in zip(whole, states)
                for f in range(2)
            ]
            numers = [dot(q, s, 1, 0) for q, _, s in parts]
            dns = []
            for (_, g, _), numer in zip(parts, numers):
                inv = 1.0 / (numer[:, HD : HD + 1] + numer[:, HD + 2 : HD + 3])
                dd = -(jnp.sum(g * numer, axis=1, keepdims=True) * inv) * inv
                hi = dd.astype(BF16).astype(F32)
                wide = jnp.where((lanes == HD) | (lanes == HD + 2), hi, g * inv)
                dns.append(jnp.where(lanes == HD + 1, dd - hi, wide).astype(BF16))
            grads = [
                (dot(dn, s, 1, 1) * jnp.minimum(q.astype(F32), 1.0)).astype(BF16) for (q, _, s), dn in zip(parts, dns)
            ]
            both = [
                dot(q, jnp.concatenate(dns[2 * u : 2 * u + 2], axis=0), 0, 0)[:HD] for u, (q, _) in enumerate(whole)
            ]
            lone = [dot(parts[2 * u][0], dns[2 * u], 0, 0)[:HD] for u in range(GROUP)]
            for u, h in enumerate(heads):
                loc[NCH + c, 0, head_rows(h, HD)] = both[u]
                loc[NCH + c, 1, head_rows(h, HD)] = lone[u]
                gp[c * CHUNK_HEADS + h] = jnp.concatenate(grads[2 * u : 2 * u + 2], axis=0)
            return 0

        lax.fori_loop(n, n + 1, some, 0)
        if n == CHUNK_HEADS // GROUP - 1:
            exchange(NCH + c)

    def keys(c):
        def some(n, _):
            heads = [n * GROUP + u for u in range(GROUP)]
            whole = [(kp[c * CHUNK_HEADS + h], vp[c * CHUNK_HEADS + h]) for h in heads]
            states = []
            for h in heads:
                first = gbuf[NCH + c, 0, head_rows(h, LANES)]
                lone = gbuf[NCH + c, 1, head_rows(h, LANES)]
                states.append((first, pack(first.astype(F32) - bs * lone.astype(F32), 1)))
            outs = []
            for (k, v), s in zip(whole, states):
                kg = jnp.concatenate(
                    [dot(v[f * HALFTOK : (f + 1) * HALFTOK], s[f], 1, 1) for f in range(2)], axis=0
                )
                vg = jnp.concatenate(
                    [dot(k[f * HALFTOK : (f + 1) * HALFTOK], s[f], 1, 0) for f in range(2)], axis=0
                )
                outs.append(((kg * jnp.minimum(k.astype(F32), 1.0)).astype(BF16), vg.astype(BF16)))
            for h, (kg, vg) in zip(heads, outs):
                kp[c * CHUNK_HEADS + h] = kg
                vp[c * CHUNK_HEADS + h] = vg
            return 0

        lax.fori_loop(0, CHUNK_HEADS // GROUP, some, 0)

    def write(src, dst, heads):
        for h in heads:
            dst[:, h * HD : (h + 1) * HD] = src[h, :, 0:HD]

    def prepare_queries():
        loads[2].wait()
        loads[3].wait()
        for c in range(NCH):
            prepare(q_in, qp, chunk[c], zero, True)
            prepare(g_in, gp, chunk[c], zero, False)

    def conv_loads():
        for n in (4, 5, 6):
            loads[n].wait()

    half = tiles // 2

    @pl.when(first_core)
    def _():
        a, b = pairs[0], pairs[1]
        a.scatter()
        b.scatter()
        prepare_queries()
        a.relay()
        b.relay()
        a.close()
        b.close()
        halo_start(1)
        conv_loads()
        halo_wait(0)
        conv(0, 0, half)
        a.over_y()
        b.over_y()
        conv(0, half, tiles)
        a.over_x()
        b.over_x()
        a.pass_on()
        b.pass_on()
        halo_wait(1)
        conv(1, 0, half)
        a.gather()

    @pl.when(second_core)
    def _():
        a, b = lones[0], lones[1]
        prepare_queries()
        a.scatter()
        b.scatter()
        conv_loads()
        a.relay()
        b.relay()
        halo_start(1)
        a.close()
        b.close()
        halo_wait(0)
        conv(0, 0, half)
        a.pass_on()
        b.pass_on()
        conv(0, half, tiles)
        a.gather()
        b.gather()
        halo_wait(1)
        conv(1, 0, tiles)

    def finish(i):
        @pl.when(first_core)
        def _():
            lones[i].finish()

        @pl.when(second_core)
        def _():
            pairs[i].finish()

    finish(0)
    queries(0, 0)
    pl.when(first_core)(pairs[1].gather)
    queries(0, 1)
    finish(1)
    queries(1, 0)
    pl.when(first_core)(pairs[NCH].scatter)
    queries(1, 1)

    @pl.when(first_core)
    def _():
        a, b = pairs[NCH], pairs[NCH + 1]
        b.scatter()
        conv(1, half, tiles)
        ksum.exchange_copy().start()
        a.relay()
        b.relay()
        a.close()
        b.close()
        write(gp, qo, chunk[0])
        a.over_y()
        b.over_y()
        write(gp, qo, chunk[1])
        a.over_x()
        b.over_x()
        a.pass_on()
        b.pass_on()
        a.gather()

    @pl.when(second_core)
    def _():
        a, b = lones[NCH], lones[NCH + 1]
        write(gp, qo, chunk[0])
        write(gp, qo, chunk[1])
        a.scatter()
        b.scatter()
        a.relay()
        b.relay()
        ksum.scatter()
        a.close()
        b.close()
        ksum.relay()
        a.pass_on()
        b.pass_on()
        ksum.close()
        a.gather()
        b.gather()
        ksum.over_y()
        ksum.over_x()
        ksum.pass_on()

    for c in range(NCH):
        finish(NCH + c)
        keys(c)
        if c == 0:
            pl.when(first_core)(pairs[NCH + 1].gather)
            pl.when(second_core)(ksum.gather)
        write(kp, ko, chunk[c])
        write(vp, vo, chunk[c])

    @pl.when(first_core)
    def _():
        ksum.finish()

    for n in range(tiles):
        wo[:, n * LANES : (n + 1) * LANES] = kgbuf[n * 16 : n * 16 + 16].astype(F32)[:9] * scale

    @pl.when(first_core)
    def _():
        for s in pairs:
            s.exchange_copy().wait_send()
            s.drain()
        ksum.exchange_copy().wait_send()

    @pl.when(second_core)
    def _():
        for s in lones:
            s.exchange_copy().wait_send()
            s.drain()
        ksum.drain()

    for f in range(2):

        @pl.when(has_next)
        def _():
            halo_copy(0, f).wait_send()

        @pl.when(has_prev)
        def _():
            halo_copy(1, f).wait_send()


def move(*refs):
    srcs, dsts, sem = refs[:5], refs[5:10], refs[10]
    copies = [pltpu.make_async_copy(s, d, sem.at[i]) for i, (s, d) in enumerate(zip(srcs, dsts))]
    for copy in copies:
        copy.start()
    for copy in copies:
        copy.wait()


def body(queries, keys, values, out_grad, block_start, conv_input, conv_grad, conv_weight):
    frames, rows, cols, width = queries.shape
    channels = conv_grad.shape[-1]
    tokens = frames * rows * cols
    all_tokens = tokens * lax.axis_size("tm") * lax.axis_size("space")
    flat = (tokens, width)
    conv_shape = conv_grad.shape
    n = 2 * NCH
    vm, dma = pltpu.VMEM, pltpu.SemaphoreType.DMA

    def tm_bufs(lead, rows_):
        return [
            vm((*lead, rows_, LANES), F32),
            vm((*lead, rows_, LANES), BF16),
            vm((*lead, 3, rows_, LANES), BF16),
            vm((*lead, rows_, LANES), BF16),
            vm((*lead, 3, rows_, LANES), BF16),
        ]

    shapes = (
        jax.ShapeDtypeStruct(flat, BF16),
        jax.ShapeDtypeStruct(flat, BF16),
        jax.ShapeDtypeStruct(flat, BF16),
        jax.ShapeDtypeStruct(conv_shape, BF16),
        jax.ShapeDtypeStruct(conv_weight.shape, F32),
    )
    outs = pl.pallas_call(
        functools.partial(kernel, 1.0 / math.sqrt(all_tokens)),
        out_shape=[pltpu.VMEM(o.shape, o.dtype) for o in shapes],
        in_specs=[pl.BlockSpec(memory_space=pl.ANY)] * 4
        + [pl.BlockSpec(memory_space=pltpu.SMEM)]
        + [pl.BlockSpec(memory_space=pl.ANY)] * 3,
        out_specs=[pl.BlockSpec(memory_space=pltpu.VMEM)] * 5,
        scratch_shapes=[
            *[vm(flat, BF16)] * 4,
            vm(conv_shape, BF16),
            vm(conv_shape, BF16),
            vm(conv_weight.shape, F32),
            *[vm((HEADS, tokens, LANES), BF16)] * 4,
            vm((2, frames, cols, channels), BF16),
            vm((KTOT, LANES), F32),
            vm((n, 2, CROWS, LANES), F32),
            vm((n, CROWS, LANES), F32),
            vm((n, 2, CROWS, LANES), BF16),
            vm((n, CROWS, LANES), BF16),
            vm((n, 2, 4, ROWS, LANES), BF16),
            vm((n, 2, ROWS, LANES), BF16),
            *tm_bufs((n,), ROWS),
            vm((KTOT, LANES), F32),
            vm((KTOT, LANES), F32),
            vm((KTOT, LANES), BF16),
            vm((KTOT, LANES), BF16),
            vm((2, 4, KROWS, LANES), BF16),
            vm((2, KROWS, LANES), BF16),
            *tm_bufs((), KROWS),
            dma((7,)), dma((2, 2)), dma((2, 2)),
            dma((n + 1,)), dma((n + 1,)),
            dma((n + 1, 2, 4)), dma((n + 1, 2, 4)),
            dma((n + 1, 2, 4)), dma((n + 1, 2, 4)),
            dma((n + 1, 3)), dma((n + 1, 3)),
            dma((n + 1, 3)), dma((n + 1, 3)),
            dma((n + 1, 9)), dma((n + 1, 9)),
        ],
        compiler_params=pltpu.CompilerParams(
            collective_id=0, has_side_effects=True, vmem_limit_bytes=56 << 20
        ),
        cost_estimate=pl.CostEstimate(flops=500_000_000, bytes_accessed=9_000_000, transcendentals=600_000),
        name="block_backward",
    )(
        queries.reshape(flat),
        keys.reshape(flat),
        values.reshape(flat),
        out_grad.reshape(flat),
        block_start,
        conv_input,
        conv_grad,
        conv_weight,
    )
    outs = pl.pallas_call(
        move,
        out_shape=shapes,
        in_specs=[pl.BlockSpec(memory_space=pltpu.VMEM)] * 5,
        out_specs=[pl.BlockSpec(memory_space=pl.ANY)] * 5,
        scratch_shapes=[dma((5,))],
        compiler_params=pltpu.CompilerParams(vmem_limit_bytes=1 << 20),
        name="results",
    )(*outs)
    shape = (frames, rows, cols, width)
    return (outs[0].reshape(shape), outs[1].reshape(shape), outs[2].reshape(shape), outs[3], outs[4])


def solution(mesh):
    split = P("tm", "space", None, None)
    return jax.shard_map(
        body,
        mesh=mesh,
        in_specs=(split, split, split, split, P("tm"), split, split, P()),
        out_specs=(split, split, split, split, P()),
        check_vma=False,
    )
```

```python
import functools
import math

import jax
import jax.numpy as jnp
from jax import lax
from jax.experimental import pallas as pl
from jax.experimental.pallas import tpu as pltpu
from jax.sharding import PartitionSpec as P

HEADS = 20
HD = 112
LANES = 128
F32 = jnp.float32
BF16 = jnp.bfloat16
MESH = pl.DeviceIdType.MESH

CHUNK_HEADS = 10
NCH = 2
NZ = 8
NR = 4
ROWS = 144
HALF = 80
CROWS = NZ * ROWS
KROWS = 96
KTOT = NZ * KROWS
KHALF = 48
TOKENS = 128
HALFTOK = 64
GROUP = 5


def lifted(wide):
    return jnp.where(wide > 0, wide + 1.0, jnp.exp(jnp.minimum(wide, 0.0)))


def dot(a, b, ca, cb):
    return lax.dot_general(a, b, (((ca,), (cb,)), ((), ())), preferred_element_type=F32)


class Place:
    def __init__(self):
        t = lax.axis_index("tm")
        s = lax.axis_index("space")
        self.t, self.s = t, s
        self.core = lax.rem(s, 2)
        self.z = lax.div(s, 2)
        self.x = lax.div(t, NR)
        self.y = lax.rem(t, NR)
        self.sibling = (t, s + 1 - 2 * self.core)
        self.up = (t, lax.rem(s + 2, 2 * NZ))
        self.down = (t, lax.rem(s + 2 * NZ - 2, 2 * NZ))
        self.ys = [(self.x * NR + lax.rem(self.y + k, NR), s) for k in (1, 2, 3)]
        self.xs = [(lax.rem(self.x + k, NR) * NR + self.y, s) for k in (1, 2, 3)]
        self.cross = (t, lax.rem(s + 2 * NZ - 1 + 2 * self.core, 2 * NZ))
        self.prev = (t, lax.rem(s + 2 * NZ - 1, 2 * NZ))
        self.next = (t, lax.rem(s + 1, 2 * NZ))


def pack(wide, step):
    lane = lax.broadcasted_iota(jnp.int32, wide.shape, 1)
    rounded = wide.astype(BF16).astype(F32)
    rest = pltpu.roll(wide - rounded, step, 1)
    return jnp.where(lane == HD + step, wide + rest, rounded).astype(BF16)


class Sum:
    forwards = 9

    def slice_from(self, d, s, far):
        o = lax.rem(self.at.z + (NZ - s if d == 0 else s), NZ)
        return self.gbuf.at[self.sl(o, *self.part(d, far))]

    def part(self, d, far):
        if not far:
            return 0, self.rows
        return (0, self.half) if d == 0 else (self.half, self.rows - self.half)

    def peer(self, d, n):
        return (self.at.t, lax.rem(self.at.s + (2 * n if d == 0 else 2 * (NZ - n)), 2 * NZ))

    def away(self, d, n):
        return lax.rem(self.at.z + (n if d == 0 else NZ - n), NZ)

    def forwarded(self, j):
        s, d = (j + 1) // 2, (j + 1) % 2
        return self.slice_from(d, s, s == 4)

    def round(self, wide):
        return wide.astype(BF16) if self.step is None else pack(wide, self.step)

    def __init__(self, at, bufs, rows, half, step):
        self.at, self.rows, self.half, self.step = at, rows, half, step
        self.pending = []
        for name, ref in bufs.items():
            setattr(self, name, ref)

    def sl(self, o, lo=0, n=None):
        n = self.rows if n is None else n
        return pl.ds(pl.multiple_of(o * self.rows + lo, 16), n)

    def remote(self, src, dst, ss, rr, dev):
        return pltpu.make_async_remote_copy(
            src_ref=src, dst_ref=dst, send_sem=ss, recv_sem=rr, device_id=dev, device_id_type=MESH
        )

    def exchange_copy(self):
        return self.remote(self.loc, self.xbuf, self.ex_s, self.ex_r, self.at.sibling)

    def go(self, make):
        make().start()
        self.pending.append(make)

    def drain(self):
        for make in self.pending:
            make().wait_send()

    def forward_copy(self, j):
        ref = self.forwarded(j)
        return self.remote(ref, ref, self.fw_s.at[j], self.fw_r.at[j], self.at.sibling)

    def finish(self):
        for j in range(self.forwards):
            self.forward_copy(j).wait_recv()


class Tree(Sum):
    def __init__(self, at, bufs, rows, half, step, mode):
        super().__init__(at, bufs, rows, half, step)
        self.mode = mode

    def far_copy(self, d, n):
        lo, count = self.part(d, n == 4)
        return self.remote(
            self.send.at[self.sl(self.away(d, n), lo, count)],
            self.recv.at[d, n - 3, pl.ds(lo, count)],
            self.rs_s.at[d, n - 3],
            self.rs_r.at[d, n - 3],
            self.peer(d, n - 2),
        )

    def near_copy(self, d):
        return self.remote(
            self.send.at[self.sl(self.away(d, 1))], self.recv.at[d, 2], self.rs_s.at[d, 2], self.rs_r.at[d, 2], self.peer(d, 1)
        )

    def middle_copy(self, d):
        return self.remote(self.middle.at[d], self.recv.at[d, 3], self.rs_s.at[d, 3], self.rs_r.at[d, 3], self.peer(d, 2))

    def scatter(self):
        self.exchange_copy().wait_recv()
        self.send[...] = self.round(self.mine[...] + self.xbuf[...])
        for n in (4, 3):
            for d in (0, 1):
                self.go(functools.partial(self.far_copy, d, n))
        for d in (0, 1):
            self.go(functools.partial(self.near_copy, d))

    def own_part(self, o, lo=0, n=None):
        at = self.sl(o, lo, n)
        return self.mine[at] + self.xbuf[at]

    def relay(self):
        for d in (0, 1):
            self.far_copy(d, 3).wait_recv()
            self.far_copy(d, 4).wait_recv()
            o = self.away(d, 2)
            lo, n = self.part(d, True)
            at = pl.ds(lo, n)
            both = self.recv[d, 0, at].astype(F32) + self.recv[d, 1, at].astype(F32)
            self.middle[d, at] = self.round(self.own_part(o, lo, n) + both)
            lo, n = self.part(1 - d, True)
            at = pl.ds(lo, n)
            self.middle[d, at] = self.round(self.own_part(o, lo, n) + self.recv[d, 0, at].astype(F32))
            self.go(functools.partial(self.middle_copy, d))

    def tm_copy(self, axis, k):
        if axis == "y":
            return self.remote(self.ysend, self.yrecv.at[k], self.y_s.at[k], self.y_r.at[k], self.at.ys[k])
        return self.remote(self.xsend, self.xrecv.at[k], self.x_s.at[k], self.x_r.at[k], self.at.xs[k])

    def weight(self, place, k):
        if self.mode == "sum":
            return 1.0
        before = (place - (k + 1) >= 0).astype(F32)
        return before if self.mode == "prefix" else 1.0 - before

    def close(self):
        own = self.own_part(self.at.z)
        for d in (0, 1):
            self.near_copy(d).wait_recv()
            own = own + self.recv[d, 2].astype(F32)
        for d in (0, 1):
            self.middle_copy(d).wait_recv()
            own = own + self.recv[d, 3].astype(F32)
        if self.mode == "lone":
            self.publish(own)
            return
        self.own[...] = own
        self.ysend[...] = self.round(own)
        for k in (1, 0, 2):
            self.go(functools.partial(self.tm_copy, "y", k))

    def over_y(self):
        total = self.own[...]
        part = total
        for k in (0, 2, 1):
            self.tm_copy("y", k).wait_recv()
            got = self.yrecv[k].astype(F32)
            total = total + got
            part = part + self.weight(self.at.y, k) * got
        self.own[...] = part
        self.xsend[...] = self.round(total)
        for k in (1, 0, 2):
            self.go(functools.partial(self.tm_copy, "x", k))

    def over_x(self):
        part = self.own[...]
        for k in (0, 2, 1):
            self.tm_copy("x", k).wait_recv()
            part = part + self.weight(self.at.x, k) * self.xrecv[k].astype(F32)
        self.publish(part)

    def publish(self, own):
        self.gbuf[self.sl(self.at.z)] = self.round(own)
        for s in (2, 1):
            for d in (0, 1):
                self.go(functools.partial(self.gather_copy, d, s))
        self.go(functools.partial(self.forward_copy, 0))

    def gather_copy(self, d, s):
        ref = self.slice_from(d, 0 if s < 3 else 2, s == 4)
        return self.remote(ref, ref, self.ag_s.at[d, s - 1], self.ag_r.at[d, s - 1], self.peer(d, s if s < 3 else s - 2))

    def arrived_copy(self, d, s):
        ref = self.slice_from(d, s, s == 4)
        return self.remote(ref, ref, self.ag_s.at[d, s - 1], self.ag_r.at[d, s - 1], self.peer(d, 1))

    def pass_on(self):
        for d in (0, 1):
            self.arrived_copy(d, 2).wait_recv()
            for s in (4, 3):
                self.go(functools.partial(self.gather_copy, d, s))
        for s in (2, 1):
            for d in (0, 1):
                if s == 1:
                    self.arrived_copy(d, 1).wait_recv()
                self.go(functools.partial(self.forward_copy, 2 * s - 1 + d))

    def gather(self):
        for s in (3, 4):
            for d in (0, 1):
                self.arrived_copy(d, s).wait_recv()
                self.go(functools.partial(self.forward_copy, 2 * s - 1 + d))


def kernel(scale, *refs):
    (
        q_hbm, k_hbm, v_hbm, g_hbm, bs_ref, ci_hbm, cg_hbm, w_hbm,
        qo, ko, vo, io, wo,
        q_in, k_in, v_in, g_in, ci_in, cg_in, w_in,
        qp, kp, vp, gp, halo, ktaps,
        loc, xbuf, gbuf,
        dsend, drecv, dmid, down, dysend, dyrecv, dxsend, dxrecv,
        kloc, kxbuf, kgbuf, ksend, krecv, kmid, kown, kysend, kyrecv, kxsend, kxrecv,
        in_sem, halo_s, halo_r,
        ex_s, ex_r, drs_s, drs_r, dag_s, dag_r, y_s, y_r, x_s, x_r,
        fw_s, fw_r,
    ) = refs
    at = Place()
    first_core, second_core = at.core == 0, at.core == 1
    channels = io.shape[-1]
    tiles = channels // LANES

    barrier = pltpu.get_barrier_semaphore()
    others = [at.sibling, at.cross, *at.ys, *at.xs]
    others += [(at.t, lax.rem(at.s + 2 * j, 2 * NZ)) for j in (1, 2, NZ - 2, NZ - 1)]
    for dev in others:
        pl.semaphore_signal(barrier, inc=1, device_id=dev, device_id_type=MESH)

    loads = [
        pltpu.make_async_copy(src, dst, in_sem.at[i])
        for i, (src, dst) in enumerate(
            [(k_hbm, k_in), (v_hbm, v_in), (q_hbm, q_in), (g_hbm, g_in), (cg_hbm, cg_in), (ci_hbm, ci_in), (w_hbm, w_in)]
        )
    ]
    for load in loads[:2]:
        load.start()

    def tree(i, which, mode):
        return Tree(
            at,
            dict(
                loc=loc.at[i, 1 - which], mine=loc.at[i, which], xbuf=xbuf.at[i], gbuf=gbuf.at[i, which],
                send=dsend.at[i], recv=drecv.at[i], middle=dmid.at[i],
                own=down.at[i], ysend=dysend.at[i], yrecv=dyrecv.at[i], xsend=dxsend.at[i], xrecv=dxrecv.at[i],
                ex_s=ex_s.at[i], ex_r=ex_r.at[i], rs_s=drs_s.at[i], rs_r=drs_r.at[i], ag_s=dag_s.at[i], ag_r=dag_r.at[i],
                y_s=y_s.at[i], y_r=y_r.at[i], x_s=x_s.at[i], x_r=x_r.at[i], fw_s=fw_s.at[i], fw_r=fw_r.at[i],
            ),
            ROWS, HALF, 2 if i < NCH else 1, mode,
        )

    pairs = [tree(i, 0, "prefix" if i < NCH else "suffix") for i in range(2 * NCH)]
    lones = [tree(i, 1, "lone") for i in range(2 * NCH)]
    i = 2 * NCH
    ksum = Tree(
        at,
        dict(
            loc=kloc, mine=kloc, xbuf=kxbuf, gbuf=kgbuf, send=ksend, recv=krecv, middle=kmid,
            own=kown, ysend=kysend, yrecv=kyrecv, xsend=kxsend, xrecv=kxrecv,
            ex_s=ex_s.at[i], ex_r=ex_r.at[i], rs_s=drs_s.at[i], rs_r=drs_r.at[i], ag_s=dag_s.at[i], ag_r=dag_r.at[i],
            y_s=y_s.at[i], y_r=y_r.at[i], x_s=x_s.at[i], x_r=x_r.at[i], fw_s=fw_s.at[i], fw_r=fw_r.at[i],
        ),
        KROWS, KHALF, None, "sum",
    )

    lane = lax.broadcasted_iota(jnp.int32, (TOKENS, LANES), 1)
    ones = ((lane == HD) | (lane == HD + 1)).astype(F32).astype(BF16)
    zero = jnp.zeros((TOKENS, LANES), BF16)

    def prepare(src, dst, heads, fill, lift):
        for h in heads:
            part = src[:, h * HD : (h + 1) * HD]
            if lift:
                part = lifted(part.astype(F32)).astype(BF16)
            dst[h] = fill
            dst[h, :, 0:HD] = part

    for i in range(2 * NCH):
        for j in range(2):
            loc[i, j, CHUNK_HEADS * HD :, :] = jnp.zeros((CROWS - CHUNK_HEADS * HD, LANES), F32)
    kloc[tiles * 16 :, :] = jnp.zeros((KTOT - tiles * 16, LANES), F32)

    @pl.when(at.s == 0)
    def _():
        halo[0] = jnp.zeros(halo.shape[1:], BF16)

    @pl.when(at.s == 2 * NZ - 1)
    def _():
        halo[1] = jnp.zeros(halo.shape[1:], BF16)

    def halo_copy(d, f):
        return pltpu.make_async_remote_copy(
            src_ref=cg_hbm.at[f, 1 - d],
            dst_ref=halo.at[d, f],
            send_sem=halo_s.at[d, f],
            recv_sem=halo_r.at[d, f],
            device_id=at.next if d == 0 else at.prev,
            device_id_type=MESH,
        )

    has_next, has_prev = at.s < 2 * NZ - 1, at.s > 0

    def halo_start(f):
        @pl.when(has_next)
        def _():
            halo_copy(0, f).start()

        @pl.when(has_prev)
        def _():
            halo_copy(1, f).start()

    def halo_wait(f):
        @pl.when(has_prev)
        def _():
            halo_copy(0, f).wait_recv()

        @pl.when(has_next)
        def _():
            halo_copy(1, f).wait_recv()

    loads[0].wait()
    loads[1].wait()
    for load in loads[2:]:
        load.start()

    def head_rows(h, n):
        return pl.ds(pl.multiple_of(h * HD, 16), n)

    def exchange(i):
        @pl.when(first_core)
        def _():
            pairs[i].exchange_copy().start()

        @pl.when(second_core)
        def _():
            lones[i].exchange_copy().start()

    def states(c):
        def some(n, _):
            heads = [n * GROUP + u for u in range(GROUP)]
            ks = [kp[c * CHUNK_HEADS + h] for h in heads]
            vs = [vp[c * CHUNK_HEADS + h] for h in heads]
            empty = jnp.zeros((HALFTOK, LANES), BF16)
            wide = [jnp.concatenate([v, jnp.concatenate([empty, v[HALFTOK:]], axis=0)], axis=1) for v in vs]
            outs = [dot(k, w, 0, 0)[:HD] for k, w in zip(ks, wide)]
            for h, o in zip(heads, outs):
                loc[c, 0, head_rows(h, HD)] = o[:, :LANES]
                loc[c, 1, head_rows(h, HD)] = o[:, LANES:]
            return 0

        lax.fori_loop(0, CHUNK_HEADS // GROUP, some, 0)
        exchange(c)

    chunk = [range(c * CHUNK_HEADS, (c + 1) * CHUNK_HEADS) for c in range(NCH)]
    for c in range(NCH):
        prepare(k_in, kp, chunk[c], zero, True)
        prepare(v_in, vp, chunk[c], ones, False)
        if c == 0:
            pl.semaphore_wait(barrier, len(others))
            halo_start(0)
        states(c)

    col = lax.broadcasted_iota(jnp.int32, (32, LANES), 0)
    not_first, not_last = col > 0, col < 31

    def conv_tile(f, n, _):
        at_lane = pl.ds(pl.multiple_of(n * LANES, LANES), LANES)
        taps = [w_in[t : t + 1, at_lane] for t in range(9)]
        sums9 = [None] * 9
        rows = [halo[0, f, :, at_lane], cg_in[f, 0, :, at_lane], cg_in[f, 1, :, at_lane], halo[1, f, :, at_lane]]
        outs = [None, None]
        inner = [ci_in[f, r, :, at_lane].astype(F32) for r in range(2)]
        for m in range(4):
            wide = rows[m].astype(F32)
            later = jnp.where(not_last, pltpu.roll(wide, 31, 0), 0.0)
            earlier = jnp.where(not_first, pltpu.roll(wide, 1, 0), 0.0)
            for r in range(2):
                i = r + 2 - m
                if 0 <= i <= 2:
                    for j, window in enumerate((later, wide, earlier)):
                        t = 3 * i + j
                        add = taps[t] * window
                        outs[r] = add if outs[r] is None else outs[r] + add
                        prod = window * inner[r]
                        prod = prod[0:8] + prod[8:16] + (prod[16:24] + prod[24:32])
                        sums9[t] = prod if sums9[t] is None else sums9[t] + prod
        for r in range(2):
            io[f, r, :, at_lane] = outs[r].astype(BF16)
        total = jnp.concatenate(
            [jnp.sum(a, axis=0, keepdims=True) for a in sums9] + [jnp.zeros((7, LANES), F32)], axis=0
        )
        place = pl.ds(pl.multiple_of(n * 16, 16), 16)
        if f == 0:
            ktaps[place] = total
        else:
            kloc[place] = ktaps[place] + total
        return 0

    def conv(f, a, b):
        lax.fori_loop(a, b, functools.partial(conv_tile, f), 0)

    bs = bs_ref[1].astype(F32)

    def queries(c, n):
        lanes = lane[:HALFTOK]

        def some(n, _):
            heads = [n * GROUP + u for u in range(GROUP)]
            whole = [(qp[c * CHUNK_HEADS + h], gp[c * CHUNK_HEADS + h]) for h in heads]
            states = []
            for h in heads:
                last = gbuf[c, 0, head_rows(h, LANES)]
                lone = gbuf[c, 1, head_rows(h, LANES)]
                states.append((pack(last.astype(F32) - bs * lone.astype(F32), 2), last))
            parts = [
                (q[f * HALFTOK : (f + 1) * HALFTOK], g[f * HALFTOK : (f + 1) * HALFTOK].astype(F32), s[f])
                for (q, g), s in zip(whole, states)
                for f in range(2)
            ]
            numers = [dot(q, s, 1, 0) for q, _, s in parts]
            dns = []
            for (_, g, _), numer in zip(parts, numers):
                inv = 1.0 / (numer[:, HD : HD + 1] + numer[:, HD + 2 : HD + 3])
                dd = -(jnp.sum(g * numer, axis=1, keepdims=True) * inv) * inv
                hi = dd.astype(BF16).astype(F32)
                wide = jnp.where((lanes == HD) | (lanes == HD + 2), hi, g * inv)
                dns.append(jnp.where(lanes == HD + 1, dd - hi, wide).astype(BF16))
            grads = [
                (dot(dn, s, 1, 1) * jnp.minimum(q.astype(F32), 1.0)).astype(BF16) for (q, _, s), dn in zip(parts, dns)
            ]
            empty = jnp.zeros((HALFTOK, LANES), BF16)
            wide = [
                jnp.concatenate(
                    [
                        jnp.concatenate(dns[2 * u : 2 * u + 2], axis=0),
                        jnp.concatenate([dns[2 * u], empty], axis=0),
                    ],
                    axis=1,
                )
                for u in range(GROUP)
            ]
            outs = [dot(q, w, 0, 0)[:HD] for (q, _), w in zip(whole, wide)]
            for u, h in enumerate(heads):
                loc[NCH + c, 0, head_rows(h, HD)] = outs[u][:, :LANES]
                loc[NCH + c, 1, head_rows(h, HD)] = outs[u][:, LANES:]
                gp[c * CHUNK_HEADS + h] = jnp.concatenate(grads[2 * u : 2 * u + 2], axis=0)
            return 0

        lax.fori_loop(n, n + 1, some, 0)
        if n == CHUNK_HEADS // GROUP - 1:
            exchange(NCH + c)

    def keys(c):
        def some(n, _):
            heads = [n * GROUP + u for u in range(GROUP)]
            whole = [(kp[c * CHUNK_HEADS + h], vp[c * CHUNK_HEADS + h]) for h in heads]
            states = []
            for h in heads:
                first = gbuf[NCH + c, 0, head_rows(h, LANES)]
                lone = gbuf[NCH + c, 1, head_rows(h, LANES)]
                states.append((first, pack(first.astype(F32) - bs * lone.astype(F32), 1)))
            outs = []
            for (k, v), s in zip(whole, states):
                kg = jnp.concatenate(
                    [dot(v[f * HALFTOK : (f + 1) * HALFTOK], s[f], 1, 1) for f in range(2)], axis=0
                )
                vg = jnp.concatenate(
                    [dot(k[f * HALFTOK : (f + 1) * HALFTOK], s[f], 1, 0) for f in range(2)], axis=0
                )
                outs.append(((kg * jnp.minimum(k.astype(F32), 1.0)).astype(BF16), vg.astype(BF16)))
            for h, (kg, vg) in zip(heads, outs):
                kp[c * CHUNK_HEADS + h] = kg
                vp[c * CHUNK_HEADS + h] = vg
            return 0

        lax.fori_loop(0, CHUNK_HEADS // GROUP, some, 0)

    def write(src, dst, heads):
        for h in heads:
            dst[:, h * HD : (h + 1) * HD] = src[h, :, 0:HD]

    def prepare_queries():
        loads[2].wait()
        loads[3].wait()
        for c in range(NCH):
            prepare(q_in, qp, chunk[c], zero, True)
            prepare(g_in, gp, chunk[c], zero, False)

    def conv_loads():
        for n in (4, 5, 6):
            loads[n].wait()

    half = tiles // 2

    @pl.when(first_core)
    def _():
        a, b = pairs[0], pairs[1]
        a.scatter()
        b.scatter()
        prepare_queries()
        a.relay()
        b.relay()
        a.close()
        b.close()
        halo_start(1)
        conv_loads()
        halo_wait(0)
        conv(0, 0, half)
        a.over_y()
        b.over_y()
        conv(0, half, tiles)
        a.over_x()
        b.over_x()
        a.pass_on()
        b.pass_on()
        a.gather()

    @pl.when(second_core)
    def _():
        a, b = lones[0], lones[1]
        prepare_queries()
        a.scatter()
        b.scatter()
        conv_loads()
        a.relay()
        b.relay()
        halo_start(1)
        a.close()
        b.close()
        halo_wait(0)
        conv(0, 0, half)
        a.pass_on()
        b.pass_on()
        conv(0, half, tiles)
        a.gather()
        b.gather()
        halo_wait(1)
        conv(1, 0, tiles)

    def finish(i):
        @pl.when(first_core)
        def _():
            lones[i].finish()

        @pl.when(second_core)
        def _():
            pairs[i].finish()

    finish(0)
    queries(0, 0)
    pl.when(first_core)(pairs[1].gather)
    queries(0, 1)
    finish(1)
    queries(1, 0)
    pl.when(first_core)(pairs[NCH].scatter)
    queries(1, 1)

    @pl.when(first_core)
    def _():
        a, b = pairs[NCH], pairs[NCH + 1]
        halo_wait(1)
        conv(1, 0, tiles // 4)
        b.scatter()
        a.relay()
        conv(1, tiles // 4, half)
        b.relay()
        conv(1, half, tiles)
        ksum.exchange_copy().start()
        a.close()
        b.close()
        write(gp, qo, chunk[0])
        a.over_y()
        b.over_y()
        write(gp, qo, chunk[1])
        a.over_x()
        b.over_x()
        a.pass_on()
        b.pass_on()
        a.gather()

    @pl.when(second_core)
    def _():
        a, b = lones[NCH], lones[NCH + 1]
        write(gp, qo, chunk[0])
        write(gp, qo, chunk[1])
        a.scatter()
        b.scatter()
        a.relay()
        b.relay()
        ksum.scatter()
        a.close()
        b.close()
        ksum.relay()
        a.pass_on()
        b.pass_on()
        ksum.close()
        a.gather()
        b.gather()
        ksum.over_y()
        ksum.over_x()
        ksum.pass_on()

    for c in range(NCH):
        finish(NCH + c)
        keys(c)
        if c == 0:
            pl.when(first_core)(pairs[NCH + 1].gather)
            pl.when(second_core)(ksum.gather)
        write(kp, ko, chunk[c])
        write(vp, vo, chunk[c])

    @pl.when(first_core)
    def _():
        ksum.finish()

    for n in range(tiles):
        wo[:, n * LANES : (n + 1) * LANES] = kgbuf[n * 16 : n * 16 + 16].astype(F32)[:9] * scale

    @pl.when(first_core)
    def _():
        for s in pairs:
            s.exchange_copy().wait_send()
            s.drain()
        ksum.exchange_copy().wait_send()

    @pl.when(second_core)
    def _():
        for s in lones:
            s.exchange_copy().wait_send()
            s.drain()
        ksum.drain()

    for f in range(2):

        @pl.when(has_next)
        def _():
            halo_copy(0, f).wait_send()

        @pl.when(has_prev)
        def _():
            halo_copy(1, f).wait_send()


def move(*refs):
    srcs, dsts, sem = refs[:5], refs[5:10], refs[10]
    copies = [pltpu.make_async_copy(s, d, sem.at[i]) for i, (s, d) in enumerate(zip(srcs, dsts))]
    for copy in copies:
        copy.start()
    for copy in copies:
        copy.wait()


def body(queries, keys, values, out_grad, block_start, conv_input, conv_grad, conv_weight):
    frames, rows, cols, width = queries.shape
    channels = conv_grad.shape[-1]
    tokens = frames * rows * cols
    all_tokens = tokens * lax.axis_size("tm") * lax.axis_size("space")
    flat = (tokens, width)
    conv_shape = conv_grad.shape
    n = 2 * NCH
    vm, dma = pltpu.VMEM, pltpu.SemaphoreType.DMA

    def tm_bufs(lead, rows_):
        return [
            vm((*lead, rows_, LANES), F32),
            vm((*lead, rows_, LANES), BF16),
            vm((*lead, 3, rows_, LANES), BF16),
            vm((*lead, rows_, LANES), BF16),
            vm((*lead, 3, rows_, LANES), BF16),
        ]

    shapes = (
        jax.ShapeDtypeStruct(flat, BF16),
        jax.ShapeDtypeStruct(flat, BF16),
        jax.ShapeDtypeStruct(flat, BF16),
        jax.ShapeDtypeStruct(conv_shape, BF16),
        jax.ShapeDtypeStruct(conv_weight.shape, F32),
    )
    outs = pl.pallas_call(
        functools.partial(kernel, 1.0 / math.sqrt(all_tokens)),
        out_shape=[pltpu.VMEM(o.shape, o.dtype) for o in shapes],
        in_specs=[pl.BlockSpec(memory_space=pl.ANY)] * 4
        + [pl.BlockSpec(memory_space=pltpu.SMEM)]
        + [pl.BlockSpec(memory_space=pl.ANY)] * 3,
        out_specs=[pl.BlockSpec(memory_space=pltpu.VMEM)] * 5,
        scratch_shapes=[
            *[vm(flat, BF16)] * 4,
            vm(conv_shape, BF16),
            vm(conv_shape, BF16),
            vm(conv_weight.shape, F32),
            *[vm((HEADS, tokens, LANES), BF16)] * 4,
            vm((2, frames, cols, channels), BF16),
            vm((KTOT, LANES), F32),
            vm((n, 2, CROWS, LANES), F32),
            vm((n, CROWS, LANES), F32),
            vm((n, 2, CROWS, LANES), BF16),
            vm((n, CROWS, LANES), BF16),
            vm((n, 2, 4, ROWS, LANES), BF16),
            vm((n, 2, ROWS, LANES), BF16),
            *tm_bufs((n,), ROWS),
            vm((KTOT, LANES), F32),
            vm((KTOT, LANES), F32),
            vm((KTOT, LANES), BF16),
            vm((KTOT, LANES), BF16),
            vm((2, 4, KROWS, LANES), BF16),
            vm((2, KROWS, LANES), BF16),
            *tm_bufs((), KROWS),
            dma((7,)), dma((2, 2)), dma((2, 2)),
            dma((n + 1,)), dma((n + 1,)),
            dma((n + 1, 2, 4)), dma((n + 1, 2, 4)),
            dma((n + 1, 2, 4)), dma((n + 1, 2, 4)),
            dma((n + 1, 3)), dma((n + 1, 3)),
            dma((n + 1, 3)), dma((n + 1, 3)),
            dma((n + 1, 9)), dma((n + 1, 9)),
        ],
        compiler_params=pltpu.CompilerParams(
            collective_id=0, has_side_effects=True, vmem_limit_bytes=56 << 20
        ),
        cost_estimate=pl.CostEstimate(flops=500_000_000, bytes_accessed=9_000_000, transcendentals=600_000),
        name="block_backward",
    )(
        queries.reshape(flat),
        keys.reshape(flat),
        values.reshape(flat),
        out_grad.reshape(flat),
        block_start,
        conv_input,
        conv_grad,
        conv_weight,
    )
    outs = pl.pallas_call(
        move,
        out_shape=shapes,
        in_specs=[pl.BlockSpec(memory_space=pltpu.VMEM)] * 5,
        out_specs=[pl.BlockSpec(memory_space=pl.ANY)] * 5,
        scratch_shapes=[dma((5,))],
        compiler_params=pltpu.CompilerParams(vmem_limit_bytes=1 << 20),
        name="results",
    )(*outs)
    shape = (frames, rows, cols, width)
    return (outs[0].reshape(shape), outs[1].reshape(shape), outs[2].reshape(shape), outs[3], outs[4])


def solution(mesh):
    split = P("tm", "space", None, None)
    return jax.shard_map(
        body,
        mesh=mesh,
        in_specs=(split, split, split, split, P("tm"), split, split, P()),
        out_specs=(split, split, split, split, P()),
        check_vma=False,
    )
```
